32 devices in a mesh: row: 8 (over z, x), vec: 4 (over y, core).
Axes of the slice: x: 2, y: 2, z: 4, core: 2. Of those that a mesh axis runs over, the one named last changes fastest.
Arguments:
- vectors: bfloat16 [8192, 1024], P(('row', 'vec')), may hold values from -6 to 6
- rotation: bfloat16 [1024, 1024], replicated, may hold values from -0.1875 to 0.1875
- blocks: bfloat16 [64, 8, 128, 128], P('row'), may hold values from -0.1875 to 0.1875
- columns: int32 [64, 8], P('row'), may hold values from 0 to 63, as said below
Outputs:
- filtered: bfloat16 [8192, 1024], P('row', 'vec')
The draws below stay inside these ranges and needn't reach their ends.
Inputs may be any that keep to these rules, and one draw needn't show every extreme that they name: `columns`: block row i stores its own block first, then block max(i - 6, 0), then block min(i + 2, 63); every other entry lies between i - 6 and i + 2, clipped to the grid.
All inputs are finite; a program needn't handle non-finite values.
Results may differ from the reference program's by a relative error of at most 0.0065.
Values may be sent and summed in bfloat16 or wider, within the bound.
A program may use at most 64 MiB of HBM per device.

```python
import jax
import jax.numpy as jnp
from jax import lax

BS = 128
NV = 1024
NNZ = 8
DEG = 4
REACH_LO = 6
REACH_HI = 2
NB = 64
NROWS = 8192


def draw_columns(key, part):
    own = jnp.arange(NB, dtype=jnp.int32)[:, None]
    offsets = jax.random.randint(key, (NB, NNZ - 3), -REACH_LO, REACH_HI + 1).astype(jnp.int32)
    fixed_part = jnp.concatenate([own, own - REACH_LO, own + REACH_HI], axis=1)
    whole = jnp.concatenate([fixed_part, own + offsets], axis=1)
    return jnp.clip(whole, 0, NB - 1).astype(jnp.int32)


def level_of(own_key, extent, cuts, smallest, largest):
    level, own = 1.0, jax.random.fold_in(own_key, 6)
    for dim, shards_of in cuts:
        heights = jnp.exp(jax.random.uniform(jax.random.fold_in(own, dim), (shards_of,), jnp.float32, smallest / len(cuts), largest / len(cuts)))
        level = level * jnp.repeat(heights, extent[dim] // shards_of).reshape([-1 if axis == dim else 1 for axis in range(len(extent))])
    return level


def normal_values(own_key, extent, deviation, reach, split=(), kind=jnp.bfloat16):
    drawn = jax.random.normal(own_key, extent, jnp.float32) * deviation
    if len(split) > 0:
        drawn = level_of(own_key, extent, split, -0.22, 0.18) * drawn
    return jnp.clip(drawn, min=-reach, max=reach).astype(kind)


def setup_inputs(seed: int = 0) -> dict:
    key_list = jax.random.split(jax.random.key(seed), 5)
    return {
        "vectors": normal_values(key_list[0], (NROWS, NV), 1.0, 6.0, ((0, 32),)),
        "rotation": normal_values(key_list[1], (NV, NV), NV ** -0.5, 0.1875),
        "blocks": normal_values(key_list[2], (NB, NNZ, BS, BS), (NNZ * BS) ** -0.5, 0.1875, ((0, 8),)),
        "columns": draw_columns(jax.random.fold_in(key_list[4], 71), 0),
    }


def apply_operator(blocks, columns, state_bf):
    tiles = state_bf.reshape(NB, BS, NV)

    def add_entry(total, entry):
        picked = tiles[columns[:, entry]].astype(jnp.float32)
        tile_ops = blocks[:, entry].astype(jnp.float32)
        return total + jnp.einsum('brc,bcv->brv', tile_ops, picked), None

    start = jnp.zeros((NB, BS, NV), jnp.float32)
    total, unused = lax.scan(add_entry, start, jnp.arange(NNZ))
    return total.reshape(NROWS, NV)


def reference(vectors, rotation, blocks, columns):
    rotated = jnp.dot(vectors, rotation, preferred_element_type=jnp.float32).astype(jnp.bfloat16)
    prev = rotated.astype(jnp.float32)
    cur = (apply_operator(blocks, columns, rotated) - 0.25 * prev) / 2.0
    for degree in range(DEG - 1):
        sent = cur.astype(jnp.bfloat16)
        nxt = 2.0 * (apply_operator(blocks, columns, sent) - 0.25 * cur) / 2.0 - prev
        prev = cur
        cur = nxt
    return cur.astype(jnp.bfloat16)
```

```python
import functools

import jax
import jax.numpy as jnp
from jax import lax
from jax.experimental import pallas as pl
from jax.experimental.pallas import tpu as pltpu
from jax.sharding import PartitionSpec as P

DEG = 4
REACH_LO = 6
REACH_HI = 2
LANES = 128
MESH = pl.DeviceIdType.MESH


def filter_kernel(
    rows, groups, halves, chunks,
    vec_hbm, rot_hbm, blk_hbm, cols_in, out_hbm,
    *scratch,
):
    refs = list(scratch)
    take = lambda n: [refs.pop(0) for _ in range(n)]
    ext = [take(halves) for _ in range(DEG)]
    state = [take(halves) for _ in range(2)]
    res = take(halves)
    vec_v, rot_v, sendbuf, blk_v, cols_v, cols_s = take(6)
    (load_sem, cols_send, cols_recv, a2a_send, a2a_recv, blk_send, blk_recv,
     fwd_send, fwd_recv, halo_send, halo_recv, out_send, out_recv) = take(13)

    local, nnz, bs, _ = blk_v.shape
    span = ext[0][0].shape[0]
    tiles, width = sendbuf.shape[2], sendbuf.shape[4]
    half_rows = local // 2
    step = half_rows // chunks

    r, v = lax.axis_index("row"), lax.axis_index("vec")
    z, x = r // 2, r % 2
    y, c = v // 2, v % 2
    s, g = 2 * z + c, 2 * y + x
    home = x == c
    away = x != c
    first = s * local

    def device_of(sup, grp):
        return (2 * (sup // 2) + grp % 2, 2 * (grp // 2) + sup % 2)

    partner = (2 * z + 1 - x, 2 * y + 1 - c)
    across = (r, 2 * (y + 1 - 2 * (y % 2)) + c)
    has_low, has_up = s > 0, s < rows - 1
    low, up = device_of(s - 1, g), device_of(s + 1, g)
    far_low = jnp.logical_and(has_low, c == 0)
    far_up = jnp.logical_and(has_up, c == 1)

    barrier = pltpu.get_barrier_semaphore()
    for k in range(1, 2 * groups):
        q = (x * groups + v + k) % (2 * groups)
        pl.semaphore_signal(
            barrier, inc=1, device_id=(2 * z + q // groups, q % groups), device_id_type=MESH)

    @pl.when(far_low)
    def _():
        pl.semaphore_signal(barrier, inc=1, device_id=low, device_id_type=MESH)

    @pl.when(far_up)
    def _():
        pl.semaphore_signal(barrier, inc=1, device_id=up, device_id_type=MESH)

    vec_copy = pltpu.make_async_copy(vec_hbm, vec_v, load_sem.at[0])
    vec_copy.start()
    rot_copies = []
    for k in range(groups):
        cols = pl.ds(pl.multiple_of(((g + 1 + k) % groups) * (halves * width), LANES), halves * width)
        rot_copies.append(
            pltpu.make_async_copy(rot_hbm.at[:, cols], rot_v.at[:, cols], load_sem.at[3 + k]))
        rot_copies[-1].start()
    blk_copy = pltpu.make_async_copy(blk_hbm, blk_v, load_sem.at[1])

    @pl.when(home)
    def _():
        blk_copy.start()

    layers = jnp.where(jnp.logical_or(far_low, far_up), 1, 0)
    pl.semaphore_wait(barrier, 2 * groups - 1 + layers)

    cols_copy = pltpu.make_async_remote_copy(
        src_ref=cols_in, dst_ref=cols_v, send_sem=cols_send, recv_sem=cols_recv,
        device_id=partner, device_id_type=MESH)

    def direct(k):
        part = pl.ds((y % 2) * half_rows + k * step, step)
        return pltpu.make_async_remote_copy(
            src_ref=blk_hbm.at[part], dst_ref=blk_v.at[part],
            send_sem=blk_send.at[k], recv_sem=blk_recv.at[k],
            device_id=partner, device_id_type=MESH)

    def forward(k, mine=True):
        side = y % 2 if mine else 1 - y % 2
        part = pl.ds(side * half_rows + k * step, step)
        return pltpu.make_async_remote_copy(
            src_ref=blk_v.at[part], dst_ref=blk_v.at[part],
            send_sem=fwd_send.at[k], recv_sem=fwd_recv.at[k],
            device_id=across, device_id_type=MESH)

    @pl.when(away)
    def _():
        cols_copy.start()
        direct(0).start()

    def a2a(grp, h):
        return pltpu.make_async_remote_copy(
            src_ref=sendbuf.at[grp, h],
            dst_ref=ext[0][h].at[pl.ds(REACH_LO + v * tiles, tiles)],
            send_sem=a2a_send.at[grp, h], recv_sem=a2a_recv.at[v, h],
            device_id=device_of(r, grp), device_id_type=MESH)

    vec_copy.wait()
    for k in range(groups):
        rot_copies[k].wait()
        grp = (g + 1 + k) % groups
        cols = pl.ds(pl.multiple_of(grp * (halves * width), LANES), halves * width)
        piece = jnp.dot(vec_v[...], rot_v[:, cols], preferred_element_type=jnp.float32)
        piece = piece.astype(jnp.bfloat16)
        own = jnp.logical_and(home, grp == g)
        for h in range(halves):
            part = piece[:, h * width:(h + 1) * width].reshape(tiles, bs, width)

            @pl.when(own)
            def _():
                ext[0][h][pl.ds(REACH_LO + v * tiles, tiles)] = part

            @pl.when(jnp.logical_not(own))
            def _():
                sendbuf[grp, h] = part
                a2a(grp, h).start()

    @pl.when(away)
    def _():
        for k in range(1, chunks):
            direct(k).start()

    def up_copy(d, h):
        return pltpu.make_async_remote_copy(
            src_ref=ext[d][h].at[pl.ds(local, REACH_LO)],
            dst_ref=ext[d][h].at[pl.ds(0, REACH_LO)],
            send_sem=halo_send.at[d, h, 0], recv_sem=halo_recv.at[d, h, 0],
            device_id=up, device_id_type=MESH)

    def down_copy(d, h):
        return pltpu.make_async_remote_copy(
            src_ref=ext[d][h].at[pl.ds(REACH_LO, REACH_HI)],
            dst_ref=ext[d][h].at[pl.ds(REACH_LO + local, REACH_HI)],
            send_sem=halo_send.at[d, h, 1], recv_sem=halo_recv.at[d, h, 1],
            device_id=low, device_id_type=MESH)

    def start_up(d, h):
        @pl.when(has_up)
        def _():
            up_copy(d, h).start()

    def start_down(d, h):
        @pl.when(has_low)
        def _():
            down_copy(d, h).start()

    def wait_halo(d, h):
        @pl.when(has_low)
        def _():
            up_copy(d, h).wait_recv()

        @pl.when(has_up)
        def _():
            down_copy(d, h).wait_recv()

    for h in range(halves):
        for src in range(groups):
            @pl.when(jnp.logical_not(jnp.logical_and(home, v == src)))
            def _():
                pltpu.make_async_remote_copy(
                    src_ref=sendbuf.at[0, h],
                    dst_ref=ext[0][h].at[pl.ds(REACH_LO + src * tiles, tiles)],
                    send_sem=a2a_send.at[0, h], recv_sem=a2a_recv.at[src, h],
                    device_id=partner, device_id_type=MESH).wait_recv()
        start_up(0, h)
        start_down(0, h)

    @pl.when(away)
    def _():
        cols_copy.wait()
        to_smem = pltpu.make_async_copy(cols_v, cols_s, load_sem.at[2])
        to_smem.start()
        to_smem.wait()
        for k in range(chunks):
            direct(k).wait_recv()
            forward(k).start()
        for k in range(chunks):
            forward(k, mine=False).wait_recv()

    @pl.when(home)
    def _():
        to_smem = pltpu.make_async_copy(cols_in, cols_s, load_sem.at[2])
        to_smem.start()
        to_smem.wait()
        blk_copy.wait()

    def apply_rows(d, h, lo, hi):
        def one_row(i, carry):
            lhs = jnp.concatenate([blk_v[i, j] for j in range(nnz)], axis=1)
            rhs = jnp.concatenate(
                [ext[d][h][jnp.clip(cols_s[i, j] - first + REACH_LO, 0, span - 1)] for j in range(nnz)],
                axis=0)
            acc = jnp.dot(lhs, rhs, preferred_element_type=jnp.float32)
            if d == 0:
                old = ext[0][h][REACH_LO + i].astype(jnp.float32)
                new = (acc - 0.25 * old) / 2.0
            else:
                cur = state[(d - 1) % 2][h][i]
                if d == 1:
                    prev = ext[0][h][REACH_LO + i].astype(jnp.float32)
                else:
                    prev = state[d % 2][h][i]
                new = (acc - 0.25 * cur) - prev
            if d < DEG - 1:
                state[d % 2][h][i] = new
                ext[d + 1][h][REACH_LO + i] = new.astype(jnp.bfloat16)
            else:
                res[h][i] = new.astype(jnp.bfloat16)
            return carry

        lax.fori_loop(lo, hi, one_row, 0, unroll=True)

    def out_part(h):
        return out_hbm.at[:, :, pl.ds(h * width, width)]

    def out_remote(h):
        return pltpu.make_async_remote_copy(
            src_ref=res[h], dst_ref=out_part(h),
            send_sem=out_send.at[h], recv_sem=out_recv.at[h],
            device_id=partner, device_id_type=MESH)

    def out_local(h):
        return pltpu.make_async_copy(res[h], out_part(h), out_send.at[h])

    for d in range(DEG):
        for h in range(halves):
            wait_halo(d, h)
            if d < DEG - 1:
                apply_rows(d, h, local - REACH_LO, local)
                start_up(d + 1, h)
                apply_rows(d, h, 0, local - REACH_LO)
                start_down(d + 1, h)
            else:
                apply_rows(d, h, 0, local)

                @pl.when(away)
                def _():
                    out_remote(h).start()

                @pl.when(home)
                def _():
                    out_local(h).start()

    for k in range(groups):
        grp = (g + 1 + k) % groups
        for h in range(halves):
            @pl.when(jnp.logical_not(jnp.logical_and(home, grp == g)))
            def _():
                a2a(grp, h).wait_send()
    for d in range(DEG):
        for h in range(halves):
            @pl.when(has_up)
            def _():
                up_copy(d, h).wait_send()

            @pl.when(has_low)
            def _():
                down_copy(d, h).wait_send()

    @pl.when(away)
    def _():
        for k in range(chunks):
            direct(k).wait_send()
            forward(k).wait_send()
        for h in range(halves):
            out_remote(h).wait()

    @pl.when(home)
    def _():
        for h in range(halves):
            out_local(h).wait()


def solution(mesh):
    rows, groups = mesh.shape["row"], mesh.shape["vec"]

    def per_device(vectors, rotation, blocks, columns):
        height, nv = vectors.shape
        local, nnz, bs, _ = blocks.shape
        group_width = nv // groups
        width = min(group_width, LANES)
        halves = group_width // width
        chunks = 4 if local % 8 == 0 else 1
        tiles = height // bs
        bf16, f32 = jnp.bfloat16, jnp.float32
        dma = pltpu.SemaphoreType.DMA
        span = REACH_LO + local + REACH_HI
        flops = 2 * height * nv * nv + 2 * DEG * local * nnz * bs * bs * group_width
        out = pl.pallas_call(
            functools.partial(filter_kernel, rows, groups, halves, chunks),
            out_shape=jax.ShapeDtypeStruct((local, bs, group_width), bf16),
            in_specs=[
                pl.BlockSpec(memory_space=pl.ANY),
                pl.BlockSpec(memory_space=pl.ANY),
                pl.BlockSpec(memory_space=pl.ANY),
                pl.BlockSpec(memory_space=pltpu.VMEM),
            ],
            out_specs=pl.BlockSpec(memory_space=pl.ANY),
            scratch_shapes=(
                [pltpu.VMEM((span, bs, width), bf16)] * (DEG * halves)
                + [pltpu.VMEM((local, bs, width), f32)] * (2 * halves)
                + [pltpu.VMEM((local, bs, width), bf16)] * halves
                + [
                    pltpu.VMEM((height, nv), bf16),
                    pltpu.VMEM((nv, nv), bf16),
                    pltpu.VMEM((groups, halves, tiles, bs, width), bf16),
                    pltpu.VMEM((local, nnz, bs, bs), bf16),
                    pltpu.VMEM(columns.shape, jnp.int32),
                    pltpu.SMEM(columns.shape, jnp.int32),
                    dma((3 + groups,)),
                    dma, dma,
                    dma((groups, halves)), dma((groups, halves)),
                    dma((chunks,)), dma((chunks,)),
                    dma((chunks,)), dma((chunks,)),
                    dma((DEG, halves, 2)), dma((DEG, halves, 2)),
                    dma((halves,)), dma((halves,)),
                ]
            ),
            compiler_params=pltpu.CompilerParams(
                collective_id=0, has_side_effects=True, vmem_limit_bytes=40 * 2**20),
            cost_estimate=pl.CostEstimate(
                flops=flops, bytes_accessed=8 * 2**20, transcendentals=0),
        )(vectors, rotation, blocks, columns)
        return out.reshape(local * bs, group_width)

    return jax.shard_map(
        per_device,
        mesh=mesh,
        in_specs=(P(("row", "vec"), None), P(), P("row", None, None, None), P("row", None)),
        out_specs=P("row", "vec"),
        check_vma=False,
    )
```

```python
import functools

import jax
import jax.numpy as jnp
from jax import lax
from jax.experimental import pallas as pl
from jax.experimental.pallas import tpu as pltpu
from jax.sharding import PartitionSpec as P

DEG = 4
REACH_LO = 6
REACH_HI = 2
LANES = 128
MESH = pl.DeviceIdType.MESH


def filter_kernel(
    rows, groups, halves, pieces,
    vec_hbm, rot_hbm, blk_hbm, cols_in, out_hbm,
    *scratch,
):
    refs = list(scratch)
    take = lambda n: [refs.pop(0) for _ in range(n)]
    ext = [take(halves) for _ in range(DEG)]
    state = [take(halves) for _ in range(2)]
    res = take(halves)
    vec_v, rot_v, sendbuf, blk_v, cols_v, cols_s = take(6)
    (load_sem, cols_send, cols_recv, a2a_send, a2a_recv, blk_send, blk_recv,
     fwd_send, fwd_recv, halo_send, halo_recv, out_send, out_recv) = take(13)

    local, nnz, bs, _ = blk_v.shape
    span = ext[0][0].shape[0]
    tiles, width = sendbuf.shape[2], sendbuf.shape[4]
    chunks = local

    r, v = lax.axis_index("row"), lax.axis_index("vec")
    z, x = r // 2, r % 2
    y, c = v // 2, v % 2
    s, g = 2 * z + c, 2 * y + x
    home = x == c
    away = x != c
    first = s * local

    def device_of(sup, grp):
        return (2 * (sup // 2) + grp % 2, 2 * (grp // 2) + sup % 2)

    partner = (2 * z + 1 - x, 2 * y + 1 - c)
    across = (r, 2 * (y + 1 - 2 * (y % 2)) + c)
    has_low, has_up = s > 0, s < rows - 1
    low, up = device_of(s - 1, g), device_of(s + 1, g)
    far_low = jnp.logical_and(has_low, c == 0)
    far_up = jnp.logical_and(has_up, c == 1)

    barrier = pltpu.get_barrier_semaphore()
    for k in range(1, 2 * groups):
        q = (x * groups + v + k) % (2 * groups)
        pl.semaphore_signal(
            barrier, inc=1, device_id=(2 * z + q // groups, q % groups), device_id_type=MESH)

    @pl.when(far_low)
    def _():
        pl.semaphore_signal(barrier, inc=1, device_id=low, device_id_type=MESH)

    @pl.when(far_up)
    def _():
        pl.semaphore_signal(barrier, inc=1, device_id=up, device_id_type=MESH)

    vec_copy = pltpu.make_async_copy(vec_hbm, vec_v, load_sem.at[0])
    vec_copy.start()
    rot_copies = []
    for k in range(groups):
        cols = pl.ds(pl.multiple_of(((g + 1 + k) % groups) * (halves * width), LANES), halves * width)
        rot_copies.append(
            pltpu.make_async_copy(rot_hbm.at[:, cols], rot_v.at[:, cols], load_sem.at[3 + k]))
        rot_copies[-1].start()
    blk_copy = pltpu.make_async_copy(blk_hbm, blk_v, load_sem.at[1])

    @pl.when(home)
    def _():
        blk_copy.start()

    layers = jnp.where(jnp.logical_or(far_low, far_up), 1, 0)
    pl.semaphore_wait(barrier, 2 * groups - 1 + layers)

    cols_copy = pltpu.make_async_remote_copy(
        src_ref=cols_in, dst_ref=cols_v, send_sem=cols_send, recv_sem=cols_recv,
        device_id=partner, device_id_type=MESH)

    def chunk(q, side):
        return (pl.ds(local - 1 - 2 * (q // 2) - side, 1), pl.ds((q % 2) * (nnz // 2), nnz // 2))

    def direct(q):
        part = chunk(q, y % 2)
        return pltpu.make_async_remote_copy(
            src_ref=blk_hbm.at[part], dst_ref=blk_v.at[part],
            send_sem=blk_send.at[q], recv_sem=blk_recv.at[q],
            device_id=partner, device_id_type=MESH)

    def forward(q, mine=True):
        part = chunk(q, y % 2 if mine else 1 - y % 2)
        return pltpu.make_async_remote_copy(
            src_ref=blk_v.at[part], dst_ref=blk_v.at[part],
            send_sem=fwd_send.at[q], recv_sem=fwd_recv.at[q],
            device_id=across, device_id_type=MESH)

    def start_direct(lo, hi):
        @pl.when(away)
        def _():
            for q in range(lo, hi):
                direct(q).start()

    def pass_on(lo, hi):
        @pl.when(away)
        def _():
            for q in range(lo, hi):
                direct(q).wait_recv()
                forward(q).start()

    @pl.when(away)
    def _():
        cols_copy.start()

    start_direct(0, 2)

    def a2a(grp, h):
        return pltpu.make_async_remote_copy(
            src_ref=sendbuf.at[grp, h],
            dst_ref=ext[0][h].at[pl.ds(REACH_LO + v * tiles, tiles)],
            send_sem=a2a_send.at[grp, h], recv_sem=a2a_recv.at[v, h],
            device_id=device_of(r, grp), device_id_type=MESH)

    vec_copy.wait()
    for k in range(groups):
        rot_copies[k].wait()
        grp = (g + 1 + k) % groups
        cols = pl.ds(pl.multiple_of(grp * (halves * width), LANES), halves * width)
        piece = jnp.dot(vec_v[...], rot_v[:, cols], preferred_element_type=jnp.float32)
        piece = piece.astype(jnp.bfloat16)
        own = jnp.logical_and(home, grp == g)
        for h in range(halves):
            part = piece[:, h * width:(h + 1) * width].reshape(tiles, bs, width)

            @pl.when(own)
            def _():
                ext[0][h][pl.ds(REACH_LO + v * tiles, tiles)] = part

            @pl.when(jnp.logical_not(own))
            def _():
                sendbuf[grp, h] = part
                a2a(grp, h).start()

    start_direct(2, 4)
    pass_on(0, 2)

    def up_copy(d, h):
        return pltpu.make_async_remote_copy(
            src_ref=ext[d][h].at[pl.ds(local, REACH_LO)],
            dst_ref=ext[d][h].at[pl.ds(0, REACH_LO)],
            send_sem=halo_send.at[d, h, 0], recv_sem=halo_recv.at[d, h, 0],
            device_id=up, device_id_type=MESH)

    def down_copy(d, h):
        return pltpu.make_async_remote_copy(
            src_ref=ext[d][h].at[pl.ds(REACH_LO, REACH_HI)],
            dst_ref=ext[d][h].at[pl.ds(REACH_LO + local, REACH_HI)],
            send_sem=halo_send.at[d, h, 1], recv_sem=halo_recv.at[d, h, 1],
            device_id=low, device_id_type=MESH)

    def start_up(d, h):
        @pl.when(has_up)
        def _():
            up_copy(d, h).start()

    def start_down(d, h):
        @pl.when(has_low)
        def _():
            down_copy(d, h).start()

    def wait_halo(d, h):
        @pl.when(has_low)
        def _():
            up_copy(d, h).wait_recv()

        @pl.when(has_up)
        def _():
            down_copy(d, h).wait_recv()

    for h in range(halves):
        for src in range(groups):
            @pl.when(jnp.logical_not(jnp.logical_and(home, v == src)))
            def _():
                pltpu.make_async_remote_copy(
                    src_ref=sendbuf.at[0, h],
                    dst_ref=ext[0][h].at[pl.ds(REACH_LO + src * tiles, tiles)],
                    send_sem=a2a_send.at[0, h], recv_sem=a2a_recv.at[src, h],
                    device_id=partner, device_id_type=MESH).wait_recv()
        start_up(0, h)
        start_down(0, h)
        if h == 0:
            start_direct(4, 6)
    start_direct(6, chunks)
    pass_on(2, 6)

    @pl.when(away)
    def _():
        cols_copy.wait()
        to_smem = pltpu.make_async_copy(cols_v, cols_s, load_sem.at[2])
        to_smem.start()
        to_smem.wait()

    @pl.when(home)
    def _():
        to_smem = pltpu.make_async_copy(cols_in, cols_s, load_sem.at[2])
        to_smem.start()
        to_smem.wait()
        blk_copy.wait()

    def one_row(d, h, i):
        lhs = jnp.concatenate([blk_v[i, j] for j in range(nnz)], axis=1)
        rhs = jnp.concatenate(
            [ext[d][h][jnp.clip(cols_s[i, j] - first + REACH_LO, 0, span - 1)] for j in range(nnz)],
            axis=0)
        acc = jnp.dot(lhs, rhs, preferred_element_type=jnp.float32)
        if d == 0:
            old = ext[0][h][REACH_LO + i].astype(jnp.float32)
            new = (acc - 0.25 * old) / 2.0
        else:
            cur = state[(d - 1) % 2][h][i]
            if d == 1:
                prev = ext[0][h][REACH_LO + i].astype(jnp.float32)
            else:
                prev = state[d % 2][h][i]
            new = (acc - 0.25 * cur) - prev
        if d < DEG - 1:
            state[d % 2][h][i] = new
            ext[d + 1][h][REACH_LO + i] = new.astype(jnp.bfloat16)
        else:
            res[h][i] = new.astype(jnp.bfloat16)

    def apply_rows(d, h, lo, hi):
        def body(i, carry):
            one_row(d, h, i)
            return carry

        lax.fori_loop(lo, hi, body, 0, unroll=True)

    def out_part(h, k):
        part = pl.ds(k * (local // pieces), local // pieces)
        return res[h].at[part], out_hbm.at[part, :, pl.ds(h * width, width)]

    def out_remote(h, k):
        src, dst = out_part(h, k)
        return pltpu.make_async_remote_copy(
            src_ref=src, dst_ref=dst, send_sem=out_send.at[h, k], recv_sem=out_recv.at[h, k],
            device_id=partner, device_id_type=MESH)

    def out_local(h, k):
        src, dst = out_part(h, k)
        return pltpu.make_async_copy(src, dst, out_send.at[h, k])

    for h in range(halves):
        wait_halo(0, h)
    for k in range(local // 2):
        if 2 * k + 2 == chunks - 2:
            pass_on(6, chunks)
        for other in (False, True):
            if other:
                @pl.when(away)
                def _():
                    for q in (2 * k, 2 * k + 1):
                        forward(q, mine=False).wait_recv()
            row = local - 1 - 2 * k - (1 - y % 2 if other else y % 2)
            for h in range(halves):
                one_row(0, h, row)
        if 2 * k + 2 == REACH_LO:
            for h in range(halves):
                start_up(1, h)
    for h in range(halves):
        start_down(1, h)

    for d in range(1, DEG):
        for h in range(halves):
            wait_halo(d, h)
            if d < DEG - 1:
                apply_rows(d, h, local - REACH_LO, local)
                start_up(d + 1, h)
                apply_rows(d, h, 0, local - REACH_LO)
                start_down(d + 1, h)
            else:
                for k in range(pieces):
                    apply_rows(d, h, k * (local // pieces), (k + 1) * (local // pieces))

                    @pl.when(away)
                    def _():
                        out_remote(h, k).start()

                    @pl.when(home)
                    def _():
                        out_local(h, k).start()

    for k in range(groups):
        grp = (g + 1 + k) % groups
        for h in range(halves):
            @pl.when(jnp.logical_not(jnp.logical_and(home, grp == g)))
            def _():
                a2a(grp, h).wait_send()
    for d in range(DEG):
        for h in range(halves):
            @pl.when(has_up)
            def _():
                up_copy(d, h).wait_send()

            @pl.when(has_low)
            def _():
                down_copy(d, h).wait_send()

    @pl.when(away)
    def _():
        for k in range(chunks):
            direct(k).wait_send()
            forward(k).wait_send()
        for h in range(halves):
            for k in range(pieces):
                out_remote(h, k).wait()

    @pl.when(home)
    def _():
        for h in range(halves):
            for k in range(pieces):
                out_local(h, k).wait()


def solution(mesh):
    rows, groups = mesh.shape["row"], mesh.shape["vec"]

    def per_device(vectors, rotation, blocks, columns):
        height, nv = vectors.shape
        local, nnz, bs, _ = blocks.shape
        group_width = nv // groups
        width = min(group_width, LANES)
        halves = group_width // width
        pieces, chunks = 2, local
        tiles = height // bs
        bf16, f32 = jnp.bfloat16, jnp.float32
        dma = pltpu.SemaphoreType.DMA
        span = REACH_LO + local + REACH_HI
        flops = 2 * height * nv * nv + 2 * DEG * local * nnz * bs * bs * group_width
        out = pl.pallas_call(
            functools.partial(filter_kernel, rows, groups, halves, pieces),
            out_shape=jax.ShapeDtypeStruct((local, bs, group_width), bf16),
            in_specs=[
                pl.BlockSpec(memory_space=pltpu.HBM),
                pl.BlockSpec(memory_space=pltpu.HBM),
                pl.BlockSpec(memory_space=pltpu.HBM),
                pl.BlockSpec(memory_space=pltpu.VMEM),
            ],
            out_specs=pl.BlockSpec(memory_space=pltpu.HBM),
            scratch_shapes=(
                [pltpu.VMEM((span, bs, width), bf16)] * (DEG * halves)
                + [pltpu.VMEM((local, bs, width), f32)] * (2 * halves)
                + [pltpu.VMEM((local, bs, width), bf16)] * halves
                + [
                    pltpu.VMEM((height, nv), bf16),
                    pltpu.VMEM((nv, nv), bf16),
                    pltpu.VMEM((groups, halves, tiles, bs, width), bf16),
                    pltpu.VMEM((local, nnz, bs, bs), bf16),
                    pltpu.VMEM(columns.shape, jnp.int32),
                    pltpu.SMEM(columns.shape, jnp.int32),
                    dma((3 + groups,)),
                    dma, dma,
                    dma((groups, halves)), dma((groups, halves)),
                    dma((chunks,)), dma((chunks,)),
                    dma((chunks,)), dma((chunks,)),
                    dma((DEG, halves, 2)), dma((DEG, halves, 2)),
                    dma((halves, pieces)), dma((halves, pieces)),
                ]
            ),
            compiler_params=pltpu.CompilerParams(
                collective_id=0, has_side_effects=True, vmem_limit_bytes=40 * 2**20),
            cost_estimate=pl.CostEstimate(
                flops=flops, bytes_accessed=8 * 2**20, transcendentals=0),
        )(vectors, rotation, blocks, columns)
        return out.reshape(local * bs, group_width)

    return jax.shard_map(
        per_device,
        mesh=mesh,
        in_specs=(P(("row", "vec"), None), P(), P("row", None, None, None), P("row", None)),
        out_specs=P("row", "vec"),
        check_vma=False,
    )
```

```python
import functools

import jax
import jax.numpy as jnp
from jax import lax
from jax.experimental import pallas as pl
from jax.experimental.pallas import tpu as pltpu
from jax.sharding import PartitionSpec as P

DEG = 4
REACH_LO = 6
REACH_HI = 2
LANES = 128
MESH = pl.DeviceIdType.MESH


def filter_kernel(
    rows, groups, halves, pieces,
    vec_hbm, rot_hbm, blk_hbm, cols_in, out_hbm,
    *scratch,
):
    refs = list(scratch)
    take = lambda n: [refs.pop(0) for _ in range(n)]
    ext = [take(halves) for _ in range(DEG)]
    state = [take(halves) for _ in range(2)]
    res = take(halves)
    vec_v, rot_v, sendbuf, blk_v, cols_v, cols_s = take(6)
    (load_sem, cols_send, cols_recv, a2a_send, a2a_recv, blk_send, blk_recv,
     fwd_send, fwd_recv, halo_send, halo_recv, out_send, out_recv) = take(13)

    local, nnz, bs, _ = blk_v.shape
    span = ext[0][0].shape[0]
    tiles, width = sendbuf.shape[2], sendbuf.shape[4]
    chunks = local

    r, v = lax.axis_index("row"), lax.axis_index("vec")
    z, x = r // 2, r % 2
    y, c = v // 2, v % 2
    s, g = 2 * z + c, 2 * y + x
    home = x == c
    away = x != c
    first = s * local

    def device_of(sup, grp):
        return (2 * (sup // 2) + grp % 2, 2 * (grp // 2) + sup % 2)

    partner = (2 * z + 1 - x, 2 * y + 1 - c)
    across = (r, 2 * (y + 1 - 2 * (y % 2)) + c)
    has_low, has_up = s > 0, s < rows - 1
    low, up = device_of(s - 1, g), device_of(s + 1, g)
    far_low = jnp.logical_and(has_low, c == 0)
    far_up = jnp.logical_and(has_up, c == 1)

    barrier = pltpu.get_barrier_semaphore()
    for k in range(1, 2 * groups):
        q = (x * groups + v + k) % (2 * groups)
        pl.semaphore_signal(
            barrier, inc=1, device_id=(2 * z + q // groups, q % groups), device_id_type=MESH)

    @pl.when(far_low)
    def _():
        pl.semaphore_signal(barrier, inc=1, device_id=low, device_id_type=MESH)

    @pl.when(far_up)
    def _():
        pl.semaphore_signal(barrier, inc=1, device_id=up, device_id_type=MESH)

    vec_copy = pltpu.make_async_copy(vec_hbm, vec_v, load_sem.at[0])
    vec_copy.start()
    rot_copies = []
    for k in range(groups):
        cols = pl.ds(pl.multiple_of(((g + 1 + k) % groups) * (halves * width), LANES), halves * width)
        rot_copies.append(
            pltpu.make_async_copy(rot_hbm.at[:, cols], rot_v.at[:, cols], load_sem.at[3 + k]))
        rot_copies[-1].start()
    blk_copy = pltpu.make_async_copy(blk_hbm, blk_v, load_sem.at[1])

    @pl.when(home)
    def _():
        blk_copy.start()

    layers = jnp.where(jnp.logical_or(far_low, far_up), 1, 0)
    pl.semaphore_wait(barrier, 2 * groups - 1 + layers)

    cols_copy = pltpu.make_async_remote_copy(
        src_ref=cols_in, dst_ref=cols_v, send_sem=cols_send, recv_sem=cols_recv,
        device_id=partner, device_id_type=MESH)

    def chunk(q, side):
        return (pl.ds(local - 1 - 2 * (q // 2) - side, 1), pl.ds((q % 2) * (nnz // 2), nnz // 2))

    def direct(q):
        part = chunk(q, y % 2)
        return pltpu.make_async_remote_copy(
            src_ref=blk_hbm.at[part], dst_ref=blk_v.at[part],
            send_sem=blk_send.at[q], recv_sem=blk_recv.at[q],
            device_id=partner, device_id_type=MESH)

    def forward(q, mine=True):
        part = chunk(q, y % 2 if mine else 1 - y % 2)
        return pltpu.make_async_remote_copy(
            src_ref=blk_v.at[part], dst_ref=blk_v.at[part],
            send_sem=fwd_send.at[q], recv_sem=fwd_recv.at[q],
            device_id=across, device_id_type=MESH)

    def start_direct(lo, hi):
        @pl.when(away)
        def _():
            for q in range(lo, hi):
                direct(q).start()

    def pass_on(lo, hi):
        @pl.when(away)
        def _():
            for q in range(lo, hi):
                direct(q).wait_recv()
                forward(q).start()

    @pl.when(away)
    def _():
        cols_copy.start()

    start_direct(0, 2)

    def a2a(grp, h):
        return pltpu.make_async_remote_copy(
            src_ref=sendbuf.at[grp, h],
            dst_ref=ext[0][h].at[pl.ds(REACH_LO + v * tiles, tiles)],
            send_sem=a2a_send.at[grp, h], recv_sem=a2a_recv.at[v, h],
            device_id=device_of(r, grp), device_id_type=MESH)

    vec_copy.wait()
    for k in range(groups):
        rot_copies[k].wait()
        grp = (g + 1 + k) % groups
        cols = pl.ds(pl.multiple_of(grp * (halves * width), LANES), halves * width)
        piece = jnp.dot(vec_v[...], rot_v[:, cols], preferred_element_type=jnp.float32)
        piece = piece.astype(jnp.bfloat16)
        own = jnp.logical_and(home, grp == g)
        for h in range(halves):
            part = piece[:, h * width:(h + 1) * width].reshape(tiles, bs, width)

            @pl.when(own)
            def _():
                ext[0][h][pl.ds(REACH_LO + v * tiles, tiles)] = part

            @pl.when(jnp.logical_not(own))
            def _():
                sendbuf[grp, h] = part
                a2a(grp, h).start()

    start_direct(2, 4)
    pass_on(0, 2)

    def up_copy(d, h):
        return pltpu.make_async_remote_copy(
            src_ref=ext[d][h].at[pl.ds(local, REACH_LO)],
            dst_ref=ext[d][h].at[pl.ds(0, REACH_LO)],
            send_sem=halo_send.at[d, h, 0], recv_sem=halo_recv.at[d, h, 0],
            device_id=up, device_id_type=MESH)

    def down_copy(d, h):
        return pltpu.make_async_remote_copy(
            src_ref=ext[d][h].at[pl.ds(REACH_LO, REACH_HI)],
            dst_ref=ext[d][h].at[pl.ds(REACH_LO + local, REACH_HI)],
            send_sem=halo_send.at[d, h, 1], recv_sem=halo_recv.at[d, h, 1],
            device_id=low, device_id_type=MESH)

    def start_up(d, h):
        @pl.when(has_up)
        def _():
            up_copy(d, h).start()

    def start_down(d, h):
        @pl.when(has_low)
        def _():
            down_copy(d, h).start()

    def wait_halo(d, h):
        @pl.when(has_low)
        def _():
            up_copy(d, h).wait_recv()

        @pl.when(has_up)
        def _():
            down_copy(d, h).wait_recv()

    for h in range(halves):
        for src in range(groups):
            @pl.when(jnp.logical_not(jnp.logical_and(home, v == src)))
            def _():
                pltpu.make_async_remote_copy(
                    src_ref=sendbuf.at[0, h],
                    dst_ref=ext[0][h].at[pl.ds(REACH_LO + src * tiles, tiles)],
                    send_sem=a2a_send.at[0, h], recv_sem=a2a_recv.at[src, h],
                    device_id=partner, device_id_type=MESH).wait_recv()
        start_up(0, h)
        start_down(0, h)
        if h == 0:
            start_direct(4, 6)
    start_direct(6, chunks)
    pass_on(2, 6)

    @pl.when(away)
    def _():
        cols_copy.wait()
        to_smem = pltpu.make_async_copy(cols_v, cols_s, load_sem.at[2])
        to_smem.start()
        to_smem.wait()

    @pl.when(home)
    def _():
        to_smem = pltpu.make_async_copy(cols_in, cols_s, load_sem.at[2])
        to_smem.start()
        to_smem.wait()
        blk_copy.wait()

    def one_row(d, h, i):
        lhs = jnp.concatenate([blk_v[i, j] for j in range(nnz)], axis=1)
        rhs = jnp.concatenate(
            [ext[d][h][jnp.clip(cols_s[i, j] - first + REACH_LO, 0, span - 1)] for j in range(nnz)],
            axis=0)
        acc = jnp.dot(lhs, rhs, preferred_element_type=jnp.float32)
        if d == 0:
            old = ext[0][h][REACH_LO + i].astype(jnp.float32)
            new = (acc - 0.25 * old) / 2.0
        else:
            cur = state[(d - 1) % 2][h][i]
            if d == 1:
                prev = ext[0][h][REACH_LO + i].astype(jnp.float32)
            else:
                prev = state[d % 2][h][i]
            new = (acc - 0.25 * cur) - prev
        if d < DEG - 1:
            state[d % 2][h][i] = new
            ext[d + 1][h][REACH_LO + i] = new.astype(jnp.bfloat16)
        else:
            res[h][i] = new.astype(jnp.bfloat16)

    def apply_rows(d, h, lo, hi):
        def body(i, carry):
            one_row(d, h, i)
            return carry

        lax.fori_loop(lo, hi, body, 0, unroll=True)

    def out_part(h, k):
        part = pl.ds(k * (local // pieces), local // pieces)
        return res[h].at[part], out_hbm.at[part, :, pl.ds(h * width, width)]

    def out_remote(h, k):
        src, dst = out_part(h, k)
        return pltpu.make_async_remote_copy(
            src_ref=src, dst_ref=dst, send_sem=out_send.at[h, k], recv_sem=out_recv.at[h, k],
            device_id=partner, device_id_type=MESH)

    def out_local(h, k):
        src, dst = out_part(h, k)
        return pltpu.make_async_copy(src, dst, out_send.at[h, k])

    for h in range(halves):
        wait_halo(0, h)
    for k in range(local // 2):
        if 2 * k + 2 == chunks - 2:
            pass_on(6, chunks)
        for other in (False, True):
            if other:
                @pl.when(away)
                def _():
                    for q in (2 * k, 2 * k + 1):
                        forward(q, mine=False).wait_recv()
            row = local - 1 - 2 * k - (1 - y % 2 if other else y % 2)
            for h in range(halves):
                one_row(0, h, row)
        if 2 * k + 2 == REACH_LO:
            for h in range(halves):
                start_up(1, h)
    for h in range(halves):
        start_down(1, h)

    for d in range(1, DEG):
        for h in range(halves):
            wait_halo(d, h)
            if d < DEG - 1:
                apply_rows(d, h, local - REACH_LO, local)
                start_up(d + 1, h)
                apply_rows(d, h, 0, local - REACH_LO)
                start_down(d + 1, h)
            else:
                for k in range(pieces):
                    apply_rows(d, h, k * (local // pieces), (k + 1) * (local // pieces))

                    @pl.when(away)
                    def _():
                        out_remote(h, k).start()

                    @pl.when(home)
                    def _():
                        out_local(h, k).start()

    for k in range(groups):
        grp = (g + 1 + k) % groups
        for h in range(halves):
            @pl.when(jnp.logical_not(jnp.logical_and(home, grp == g)))
            def _():
                a2a(grp, h).wait_send()
    for d in range(DEG):
        for h in range(halves):
            @pl.when(has_up)
            def _():
                up_copy(d, h).wait_send()

            @pl.when(has_low)
            def _():
                down_copy(d, h).wait_send()

    @pl.when(away)
    def _():
        for k in range(chunks):
            direct(k).wait_send()
            forward(k).wait_send()
        for h in range(halves):
            for k in range(pieces):
                out_remote(h, k).wait()

    @pl.when(home)
    def _():
        for h in range(halves):
            for k in range(pieces):
                out_local(h, k).wait()


def solution(mesh):
    rows, groups = mesh.shape["row"], mesh.shape["vec"]

    def per_device(vectors, rotation, blocks, columns):
        height, nv = vectors.shape
        local, nnz, bs, _ = blocks.shape
        group_width = nv // groups
        width = min(group_width, LANES)
        halves = group_width // width
        pieces, chunks = 2, local
        tiles = height // bs
        bf16, f32 = jnp.bfloat16, jnp.float32
        dma = pltpu.SemaphoreType.DMA
        span = REACH_LO + local + REACH_HI
        flops = 2 * height * nv * nv + 2 * DEG * local * nnz * bs * bs * group_width
        out = pl.pallas_call(
            functools.partial(filter_kernel, rows, groups, halves, pieces),
            out_shape=jax.ShapeDtypeStruct((local, bs, group_width), bf16),
            in_specs=[
                pl.BlockSpec(memory_space=pl.ANY),
                pl.BlockSpec(memory_space=pl.ANY),
                pl.BlockSpec(memory_space=pl.ANY),
                pl.BlockSpec(memory_space=pl.ANY),
            ],
            out_specs=pl.BlockSpec(memory_space=pl.ANY),
            scratch_shapes=(
                [pltpu.VMEM((span, bs, width), bf16)] * (DEG * halves)
                + [pltpu.VMEM((local, bs, width), f32)] * (2 * halves)
                + [pltpu.VMEM((local, bs, width), bf16)] * halves
                + [
                    pltpu.VMEM((height, nv), bf16),
                    pltpu.VMEM((nv, nv), bf16),
                    pltpu.VMEM((groups, halves, tiles, bs, width), bf16),
                    pltpu.VMEM((local, nnz, bs, bs), bf16),
                    pltpu.VMEM(columns.shape, jnp.int32),
                    pltpu.SMEM(columns.shape, jnp.int32),
                    dma((3 + groups,)),
                    dma, dma,
                    dma((groups, halves)), dma((groups, halves)),
                    dma((chunks,)), dma((chunks,)),
                    dma((chunks,)), dma((chunks,)),
                    dma((DEG, halves, 2)), dma((DEG, halves, 2)),
                    dma((halves, pieces)), dma((halves, pieces)),
                ]
            ),
            compiler_params=pltpu.CompilerParams(
                collective_id=0, has_side_effects=True, vmem_limit_bytes=127 * 2**19),
            cost_estimate=pl.CostEstimate(
                flops=flops, bytes_accessed=8 * 2**20, transcendentals=0),
        )(vectors, rotation, blocks, columns)
        return out.reshape(local * bs, group_width)

    return jax.shard_map(
        per_device,
        mesh=mesh,
        in_specs=(P(("row", "vec"), None), P(), P("row", None, None, None), P("row", None)),
        out_specs=P("row", "vec"),
        check_vma=False,
    )
```

```python
import functools

import jax
import jax.numpy as jnp
from jax import lax
from jax.experimental import pallas as pl
from jax.experimental.pallas import tpu as pltpu
from jax.sharding import PartitionSpec as P

DEG = 4
REACH_LO = 6
REACH_HI = 2
LANES = 128
MESH = pl.DeviceIdType.MESH


def filter_kernel(
    rows, groups, halves, pieces,
    vec_hbm, rot_hbm, blk_hbm, cols_in, out_hbm,
    *scratch,
):
    refs = list(scratch)
    take = lambda n: [refs.pop(0) for _ in range(n)]
    ext = [take(halves) for _ in range(DEG)]
    state = [take(halves) for _ in range(2)]
    res = take(halves)
    vec_v, rot_v, sendbuf, blk_v, cols_v, cols_s = take(6)
    (load_sem, cols_send, cols_recv, a2a_send, a2a_recv, blk_send, blk_recv,
     fwd_send, fwd_recv, halo_send, halo_recv, out_send, out_recv) = take(13)

    local, nnz, bs, _ = blk_v.shape
    span = ext[0][0].shape[0]
    tiles, width = sendbuf.shape[2], sendbuf.shape[4]
    chunks = local

    r, v = lax.axis_index("row"), lax.axis_index("vec")
    z, x = r // 2, r % 2
    y, c = v // 2, v % 2
    s, g = 2 * z + c, 2 * y + x
    home = x == c
    away = x != c
    first = s * local

    def device_of(sup, grp):
        return (2 * (sup // 2) + grp % 2, 2 * (grp // 2) + sup % 2)

    partner = (2 * z + 1 - x, 2 * y + 1 - c)
    across = (r, 2 * (y + 1 - 2 * (y % 2)) + c)
    has_low, has_up = s > 0, s < rows - 1
    low, up = device_of(s - 1, g), device_of(s + 1, g)
    far_low = jnp.logical_and(has_low, c == 0)
    far_up = jnp.logical_and(has_up, c == 1)

    barrier = pltpu.get_barrier_semaphore()
    for k in range(1, 2 * groups):
        q = (x * groups + v + k) % (2 * groups)
        pl.semaphore_signal(
            barrier, inc=1, device_id=(2 * z + q // groups, q % groups), device_id_type=MESH)

    @pl.when(far_low)
    def _():
        pl.semaphore_signal(barrier, inc=1, device_id=low, device_id_type=MESH)

    @pl.when(far_up)
    def _():
        pl.semaphore_signal(barrier, inc=1, device_id=up, device_id_type=MESH)

    vec_copy = pltpu.make_async_copy(vec_hbm, vec_v, load_sem.at[0])
    vec_copy.start()
    rot_copies = []
    for k in range(groups):
        cols = pl.ds(pl.multiple_of(((g + 1 + k) % groups) * (halves * width), LANES), halves * width)
        rot_copies.append(
            pltpu.make_async_copy(rot_hbm.at[:, cols], rot_v.at[:, cols], load_sem.at[3 + k]))
        rot_copies[-1].start()
    blk_copy = pltpu.make_async_copy(blk_hbm, blk_v, load_sem.at[1])

    @pl.when(home)
    def _():
        blk_copy.start()

    layers = jnp.where(jnp.logical_or(far_low, far_up), 1, 0)
    pl.semaphore_wait(barrier, 2 * groups - 1 + layers)

    cols_copy = pltpu.make_async_remote_copy(
        src_ref=cols_in, dst_ref=cols_v, send_sem=cols_send, recv_sem=cols_recv,
        device_id=partner, device_id_type=MESH)

    def chunk(q, side):
        return (pl.ds(local - 1 - 2 * (q // 2) - side, 1), pl.ds((q % 2) * (nnz // 2), nnz // 2))

    def direct(q):
        part = chunk(q, y % 2)
        return pltpu.make_async_remote_copy(
            src_ref=blk_hbm.at[part], dst_ref=blk_v.at[part],
            send_sem=blk_send.at[q], recv_sem=blk_recv.at[q],
            device_id=partner, device_id_type=MESH)

    def forward(q, mine=True):
        part = chunk(q, y % 2 if mine else 1 - y % 2)
        return pltpu.make_async_remote_copy(
            src_ref=blk_v.at[part], dst_ref=blk_v.at[part],
            send_sem=fwd_send.at[q], recv_sem=fwd_recv.at[q],
            device_id=across, device_id_type=MESH)

    def start_direct(lo, hi):
        @pl.when(away)
        def _():
            for q in range(lo, hi):
                direct(q).start()

    def pass_on(lo, hi):
        @pl.when(away)
        def _():
            for q in range(lo, hi):
                direct(q).wait_recv()
                forward(q).start()

    @pl.when(away)
    def _():
        cols_copy.start()

    start_direct(0, 2)

    def a2a(grp, h):
        return pltpu.make_async_remote_copy(
            src_ref=sendbuf.at[grp, h],
            dst_ref=ext[0][h].at[pl.ds(REACH_LO + v * tiles, tiles)],
            send_sem=a2a_send.at[grp, h], recv_sem=a2a_recv.at[v, h],
            device_id=device_of(r, grp), device_id_type=MESH)

    vec_copy.wait()
    for k in range(groups):
        rot_copies[k].wait()
        grp = (g + 1 + k) % groups
        cols = pl.ds(pl.multiple_of(grp * (halves * width), LANES), halves * width)
        piece = jnp.dot(vec_v[...], rot_v[:, cols], preferred_element_type=jnp.float32)
        piece = piece.astype(jnp.bfloat16)
        own = jnp.logical_and(home, grp == g)
        for h in range(halves):
            part = piece[:, h * width:(h + 1) * width].reshape(tiles, bs, width)

            @pl.when(own)
            def _():
                ext[0][h][pl.ds(REACH_LO + v * tiles, tiles)] = part

            @pl.when(jnp.logical_not(own))
            def _():
                sendbuf[grp, h] = part
                a2a(grp, h).start()

    start_direct(2, 4)
    pass_on(0, 2)

    def up_copy(d, h):
        return pltpu.make_async_remote_copy(
            src_ref=ext[d][h].at[pl.ds(local, REACH_LO)],
            dst_ref=ext[d][h].at[pl.ds(0, REACH_LO)],
            send_sem=halo_send.at[d, h, 0], recv_sem=halo_recv.at[d, h, 0],
            device_id=up, device_id_type=MESH)

    def down_copy(d, h):
        return pltpu.make_async_remote_copy(
            src_ref=ext[d][h].at[pl.ds(REACH_LO, REACH_HI)],
            dst_ref=ext[d][h].at[pl.ds(REACH_LO + local, REACH_HI)],
            send_sem=halo_send.at[d, h, 1], recv_sem=halo_recv.at[d, h, 1],
            device_id=low, device_id_type=MESH)

    def start_up(d, h):
        @pl.when(has_up)
        def _():
            up_copy(d, h).start()

    def start_down(d, h):
        @pl.when(has_low)
        def _():
            down_copy(d, h).start()

    def wait_halo(d, h):
        @pl.when(has_low)
        def _():
            up_copy(d, h).wait_recv()

        @pl.when(has_up)
        def _():
            down_copy(d, h).wait_recv()

    for h in range(halves):
        for src in range(groups):
            @pl.when(jnp.logical_not(jnp.logical_and(home, v == src)))
            def _():
                pltpu.make_async_remote_copy(
                    src_ref=sendbuf.at[0, h],
                    dst_ref=ext[0][h].at[pl.ds(REACH_LO + src * tiles, tiles)],
                    send_sem=a2a_send.at[0, h], recv_sem=a2a_recv.at[src, h],
                    device_id=partner, device_id_type=MESH).wait_recv()
        start_up(0, h)
        start_down(0, h)
        if h == 0:
            start_direct(4, 6)
    start_direct(6, chunks)
    pass_on(2, 6)

    @pl.when(away)
    def _():
        cols_copy.wait()
        to_smem = pltpu.make_async_copy(cols_v, cols_s, load_sem.at[2])
        to_smem.start()
        to_smem.wait()

    @pl.when(home)
    def _():
        to_smem = pltpu.make_async_copy(cols_in, cols_s, load_sem.at[2])
        to_smem.start()
        to_smem.wait()
        blk_copy.wait()

    def product(d, parts, i):
        lhs = jnp.concatenate([blk_v[i, j] for j in range(nnz)], axis=1)
        tile = [jnp.clip(cols_s[i, j] - first + REACH_LO, 0, span - 1) for j in range(nnz)]
        rhs = [jnp.concatenate([ext[d][h][t] for t in tile], axis=0) for h in parts]
        rhs = rhs[0] if len(parts) == 1 else jnp.concatenate(rhs, axis=1)
        return jnp.dot(lhs, rhs, preferred_element_type=jnp.float32)

    def first_row(i):
        acc = product(0, range(halves), i)
        for h in range(halves):
            old = ext[0][h][REACH_LO + i].astype(jnp.float32)
            new = (acc[:, h * width:(h + 1) * width] - 0.25 * old) / 2.0
            state[0][h][i] = new
            ext[1][h][REACH_LO + i] = new.astype(jnp.bfloat16)

    def one_row(d, h, i):
        acc = product(d, (h,), i)
        cur = state[(d - 1) % 2][h][i]
        if d == 1:
            prev = ext[0][h][REACH_LO + i].astype(jnp.float32)
        else:
            prev = state[d % 2][h][i]
        new = (acc - 0.25 * cur) - prev
        if d < DEG - 1:
            state[d % 2][h][i] = new
            ext[d + 1][h][REACH_LO + i] = new.astype(jnp.bfloat16)
        else:
            res[h][i] = new.astype(jnp.bfloat16)

    def apply_rows(d, h, lo, hi):
        def body(i, carry):
            one_row(d, h, i)
            return carry

        lax.fori_loop(lo, hi, body, 0, unroll=True)

    def out_part(h, k):
        part = pl.ds(k * (local // pieces), local // pieces)
        return res[h].at[part], out_hbm.at[h, part]

    def out_remote(h, k):
        src, dst = out_part(h, k)
        return pltpu.make_async_remote_copy(
            src_ref=src, dst_ref=dst, send_sem=out_send.at[h, k], recv_sem=out_recv.at[h, k],
            device_id=partner, device_id_type=MESH)

    def out_local(h, k):
        src, dst = out_part(h, k)
        return pltpu.make_async_copy(src, dst, out_send.at[h, k])

    for h in range(halves):
        wait_halo(0, h)
    for k in range(local // 2):
        if 2 * k + 2 == chunks - 2:
            pass_on(6, chunks)
        for other in (False, True):
            if other:
                @pl.when(away)
                def _():
                    for q in (2 * k, 2 * k + 1):
                        forward(q, mine=False).wait_recv()
            row = local - 1 - 2 * k - (1 - y % 2 if other else y % 2)
            first_row(row)
        if 2 * k + 2 == REACH_LO:
            for h in range(halves):
                start_up(1, h)
    for h in range(halves):
        start_down(1, h)

    for d in range(1, DEG):
        for h in range(halves):
            wait_halo(d, h)
            if d < DEG - 1:
                apply_rows(d, h, local - REACH_LO, local)
                start_up(d + 1, h)
                apply_rows(d, h, 0, local - REACH_LO)
                start_down(d + 1, h)
            else:
                for k in range(pieces):
                    apply_rows(d, h, k * (local // pieces), (k + 1) * (local // pieces))

                    @pl.when(away)
                    def _():
                        out_remote(h, k).start()

                    @pl.when(home)
                    def _():
                        out_local(h, k).start()

    for k in range(groups):
        grp = (g + 1 + k) % groups
        for h in range(halves):
            @pl.when(jnp.logical_not(jnp.logical_and(home, grp == g)))
            def _():
                a2a(grp, h).wait_send()
    for d in range(DEG):
        for h in range(halves):
            @pl.when(has_up)
            def _():
                up_copy(d, h).wait_send()

            @pl.when(has_low)
            def _():
                down_copy(d, h).wait_send()

    @pl.when(away)
    def _():
        for k in range(chunks):
            direct(k).wait_send()
            forward(k).wait_send()
        for h in range(halves):
            for k in range(pieces):
                out_remote(h, k).wait()

    @pl.when(home)
    def _():
        for h in range(halves):
            for k in range(pieces):
                out_local(h, k).wait()


def side_by_side(parts, whole):
    halves, rows, bs, width = parts.shape
    for h in range(halves):
        whole[:, h * width:(h + 1) * width] = parts[h].reshape(rows * bs, width)


def solution(mesh):
    rows, groups = mesh.shape["row"], mesh.shape["vec"]

    def per_device(vectors, rotation, blocks, columns):
        height, nv = vectors.shape
        local, nnz, bs, _ = blocks.shape
        group_width = nv // groups
        width = min(group_width, LANES)
        halves = group_width // width
        pieces = 2
        tiles = height // bs
        bf16, f32 = jnp.bfloat16, jnp.float32
        dma = pltpu.SemaphoreType.DMA
        span = REACH_LO + local + REACH_HI
        flops = 2 * height * nv * nv + 2 * DEG * local * nnz * bs * bs * group_width
        out = pl.pallas_call(
            functools.partial(filter_kernel, rows, groups, halves, pieces),
            out_shape=jax.ShapeDtypeStruct((halves, local, bs, width), bf16),
            in_specs=[
                pl.BlockSpec(memory_space=pl.ANY),
                pl.BlockSpec(memory_space=pl.ANY),
                pl.BlockSpec(memory_space=pl.ANY),
                pl.BlockSpec(memory_space=pl.ANY),
            ],
            out_specs=pl.BlockSpec(memory_space=pl.ANY),
            scratch_shapes=(
                [pltpu.VMEM((span, bs, width), bf16)] * (DEG * halves)
                + [pltpu.VMEM((local, bs, width), f32)] * (2 * halves)
                + [pltpu.VMEM((local, bs, width), bf16)] * halves
                + [
                    pltpu.VMEM((height, nv), bf16),
                    pltpu.VMEM((nv, nv), bf16),
                    pltpu.VMEM((groups, halves, tiles, bs, width), bf16),
                    pltpu.VMEM((local, nnz, bs, bs), bf16),
                    pltpu.VMEM(columns.shape, jnp.int32),
                    pltpu.SMEM(columns.shape, jnp.int32),
                    dma((3 + groups,)),
                    dma, dma,
                    dma((groups, halves)), dma((groups, halves)),
                    dma((local,)), dma((local,)),
                    dma((local,)), dma((local,)),
                    dma((DEG, halves, 2)), dma((DEG, halves, 2)),
                    dma((halves, pieces)), dma((halves, pieces)),
                ]
            ),
            compiler_params=pltpu.CompilerParams(
                collective_id=0, has_side_effects=True, vmem_limit_bytes=127 * 2**19),
            cost_estimate=pl.CostEstimate(
                flops=flops, bytes_accessed=8 * 2**20, transcendentals=0),
        )(vectors, rotation, blocks, columns)
        return pl.pallas_call(
            side_by_side,
            grid=(2,),
            out_shape=jax.ShapeDtypeStruct((local * bs, group_width), bf16),
            in_specs=[pl.BlockSpec((halves, local // 2, bs, width), lambda i: (0, i, 0, 0))],
            out_specs=pl.BlockSpec((local // 2 * bs, group_width), lambda i: (i, 0)),
            compiler_params=pltpu.CompilerParams(vmem_limit_bytes=8 * 2**20),
        )(out)

    return jax.shard_map(
        per_device,
        mesh=mesh,
        in_specs=(P(("row", "vec"), None), P(), P("row", None, None, None), P("row", None)),
        out_specs=P("row", "vec"),
        check_vma=False,
    )
```

```python
import functools

import jax
import jax.numpy as jnp
from jax import lax
from jax.experimental import pallas as pl
from jax.experimental.pallas import tpu as pltpu
from jax.sharding import PartitionSpec as P

DEG = 4
REACH_LO = 6
REACH_HI = 2
LANES = 128
MESH = pl.DeviceIdType.MESH


def filter_kernel(
    rows, groups, halves, pieces,
    vec_hbm, rot_hbm, blk_hbm, cols_in, out_hbm,
    *scratch,
):
    refs = list(scratch)
    take = lambda n: [refs.pop(0) for _ in range(n)]
    ext = [take(halves) for _ in range(DEG)]
    state = [take(halves) for _ in range(2)]
    res = take(halves)
    vec_v, rot_v, sendbuf, blk_v, cols_v, cols_s = take(6)
    (load_sem, cols_send, cols_recv, a2a_send, a2a_recv, blk_send, blk_recv,
     fwd_send, fwd_recv, halo_send, halo_recv, out_send, out_recv) = take(13)

    local, nnz, bs, _ = blk_v.shape
    span = ext[0][0].shape[0]
    tiles, width = sendbuf.shape[2], sendbuf.shape[4]
    chunks = local

    r, v = lax.axis_index("row"), lax.axis_index("vec")
    z, x = r // 2, r % 2
    y, c = v // 2, v % 2
    s, g = 2 * z + c, 2 * y + x
    home = x == c
    away = x != c
    first = s * local

    def device_of(sup, grp):
        return (2 * (sup // 2) + grp % 2, 2 * (grp // 2) + sup % 2)

    partner = (2 * z + 1 - x, 2 * y + 1 - c)
    across = (r, 2 * (y + 1 - 2 * (y % 2)) + c)
    has_low, has_up = s > 0, s < rows - 1
    low, up = device_of(s - 1, g), device_of(s + 1, g)
    far_low = jnp.logical_and(has_low, c == 0)
    far_up = jnp.logical_and(has_up, c == 1)

    barrier = pltpu.get_barrier_semaphore()
    for k in range(1, 2 * groups):
        q = (x * groups + v + k) % (2 * groups)
        pl.semaphore_signal(
            barrier, inc=1, device_id=(2 * z + q // groups, q % groups), device_id_type=MESH)

    @pl.when(far_low)
    def _():
        pl.semaphore_signal(barrier, inc=1, device_id=low, device_id_type=MESH)

    @pl.when(far_up)
    def _():
        pl.semaphore_signal(barrier, inc=1, device_id=up, device_id_type=MESH)

    vec_copy = pltpu.make_async_copy(vec_hbm, vec_v, load_sem.at[0])
    vec_copy.start()
    rot_copies = []
    for k in range(groups):
        cols = pl.ds(pl.multiple_of(((g + 1 + k) % groups) * (halves * width), LANES), halves * width)
        rot_copies.append(
            pltpu.make_async_copy(rot_hbm.at[:, cols], rot_v.at[:, cols], load_sem.at[3 + k]))
        rot_copies[-1].start()
    blk_copy = pltpu.make_async_copy(blk_hbm, blk_v, load_sem.at[1])

    @pl.when(home)
    def _():
        blk_copy.start()

    layers = jnp.where(jnp.logical_or(far_low, far_up), 1, 0)
    pl.semaphore_wait(barrier, 2 * groups - 1 + layers)

    cols_copy = pltpu.make_async_remote_copy(
        src_ref=cols_in, dst_ref=cols_v, send_sem=cols_send, recv_sem=cols_recv,
        device_id=partner, device_id_type=MESH)

    def chunk(q, side):
        return (pl.ds(local - 1 - 2 * (q // 2) - side, 1), pl.ds((q % 2) * (nnz // 2), nnz // 2))

    def direct(q):
        part = chunk(q, y % 2)
        return pltpu.make_async_remote_copy(
            src_ref=blk_hbm.at[part], dst_ref=blk_v.at[part],
            send_sem=blk_send.at[q], recv_sem=blk_recv.at[q],
            device_id=partner, device_id_type=MESH)

    def forward(q, mine=True):
        part = chunk(q, y % 2 if mine else 1 - y % 2)
        return pltpu.make_async_remote_copy(
            src_ref=blk_v.at[part], dst_ref=blk_v.at[part],
            send_sem=fwd_send.at[q], recv_sem=fwd_recv.at[q],
            device_id=across, device_id_type=MESH)

    def start_direct(lo, hi):
        @pl.when(away)
        def _():
            for q in range(lo, hi):
                direct(q).start()

    def pass_on(lo, hi):
        @pl.when(away)
        def _():
            for q in range(lo, hi):
                direct(q).wait_recv()
                forward(q).start()

    @pl.when(away)
    def _():
        cols_copy.start()

    start_direct(0, 3)

    def a2a(grp, h):
        return pltpu.make_async_remote_copy(
            src_ref=sendbuf.at[grp, h],
            dst_ref=ext[0][h].at[pl.ds(REACH_LO + v * tiles, tiles)],
            send_sem=a2a_send.at[grp, h], recv_sem=a2a_recv.at[v, h],
            device_id=device_of(r, grp), device_id_type=MESH)

    vec_copy.wait()
    for k in range(groups):
        rot_copies[k].wait()
        if k == groups - 1:
            pass_on(0, 1)
        grp = (g + 1 + k) % groups
        cols = pl.ds(pl.multiple_of(grp * (halves * width), LANES), halves * width)
        piece = jnp.dot(vec_v[...], rot_v[:, cols], preferred_element_type=jnp.float32)
        piece = piece.astype(jnp.bfloat16)
        own = jnp.logical_and(home, grp == g)
        for h in range(halves):
            part = piece[:, h * width:(h + 1) * width].reshape(tiles, bs, width)

            @pl.when(own)
            def _():
                ext[0][h][pl.ds(REACH_LO + v * tiles, tiles)] = part

            @pl.when(jnp.logical_not(own))
            def _():
                sendbuf[grp, h] = part
                a2a(grp, h).start()

    start_direct(3, 5)
    pass_on(1, 2)

    def up_copy(d, h):
        return pltpu.make_async_remote_copy(
            src_ref=ext[d][h].at[pl.ds(local, REACH_LO)],
            dst_ref=ext[d][h].at[pl.ds(0, REACH_LO)],
            send_sem=halo_send.at[d, h, 0], recv_sem=halo_recv.at[d, h, 0],
            device_id=up, device_id_type=MESH)

    def down_copy(d, h):
        return pltpu.make_async_remote_copy(
            src_ref=ext[d][h].at[pl.ds(REACH_LO, REACH_HI)],
            dst_ref=ext[d][h].at[pl.ds(REACH_LO + local, REACH_HI)],
            send_sem=halo_send.at[d, h, 1], recv_sem=halo_recv.at[d, h, 1],
            device_id=low, device_id_type=MESH)

    def start_up(d, h):
        @pl.when(has_up)
        def _():
            up_copy(d, h).start()

    def start_down(d, h):
        @pl.when(has_low)
        def _():
            down_copy(d, h).start()

    def wait_halo(d, h):
        @pl.when(has_low)
        def _():
            up_copy(d, h).wait_recv()

        @pl.when(has_up)
        def _():
            down_copy(d, h).wait_recv()

    for h in range(halves):
        for src in range(groups):
            @pl.when(jnp.logical_not(jnp.logical_and(home, v == src)))
            def _():
                pltpu.make_async_remote_copy(
                    src_ref=sendbuf.at[0, h],
                    dst_ref=ext[0][h].at[pl.ds(REACH_LO + src * tiles, tiles)],
                    send_sem=a2a_send.at[0, h], recv_sem=a2a_recv.at[src, h],
                    device_id=partner, device_id_type=MESH).wait_recv()
        start_up(0, h)
        start_down(0, h)
        if h == 0:
            start_direct(5, 6)
    start_direct(6, chunks)
    pass_on(2, chunks - 2)

    @pl.when(away)
    def _():
        cols_copy.wait()
        to_smem = pltpu.make_async_copy(cols_v, cols_s, load_sem.at[2])
        to_smem.start()
        to_smem.wait()

    @pl.when(home)
    def _():
        to_smem = pltpu.make_async_copy(cols_in, cols_s, load_sem.at[2])
        to_smem.start()
        to_smem.wait()
        blk_copy.wait()

    def product(d, parts, i):
        lhs = jnp.concatenate([blk_v[i, j] for j in range(nnz)], axis=1)
        tile = [jnp.clip(cols_s[i, j] - first + REACH_LO, 0, span - 1) for j in range(nnz)]
        rhs = [jnp.concatenate([ext[d][h][t] for t in tile], axis=0) for h in parts]
        rhs = rhs[0] if len(parts) == 1 else jnp.concatenate(rhs, axis=1)
        return jnp.dot(lhs, rhs, preferred_element_type=jnp.float32)

    def first_row(i):
        acc = product(0, range(halves), i)
        for h in range(halves):
            old = ext[0][h][REACH_LO + i].astype(jnp.float32)
            new = (acc[:, h * width:(h + 1) * width] - 0.25 * old) / 2.0
            state[0][h][i] = new
            ext[1][h][REACH_LO + i] = new.astype(jnp.bfloat16)

    def one_row(d, h, i):
        acc = product(d, (h,), i)
        cur = state[(d - 1) % 2][h][i]
        if d == 1:
            prev = ext[0][h][REACH_LO + i].astype(jnp.float32)
        else:
            prev = state[d % 2][h][i]
        new = (acc - 0.25 * cur) - prev
        if d < DEG - 1:
            state[d % 2][h][i] = new
            ext[d + 1][h][REACH_LO + i] = new.astype(jnp.bfloat16)
        else:
            res[h][i] = new.astype(jnp.bfloat16)

    def apply_rows(d, h, lo, hi):
        def body(i, carry):
            one_row(d, h, i)
            return carry

        lax.fori_loop(lo, hi, body, 0, unroll=True)

    def out_part(h, k):
        part = pl.ds(k * (local // pieces), local // pieces)
        return res[h].at[part], out_hbm.at[h, part]

    def out_remote(h, k):
        src, dst = out_part(h, k)
        return pltpu.make_async_remote_copy(
            src_ref=src, dst_ref=dst, send_sem=out_send.at[h, k], recv_sem=out_recv.at[h, k],
            device_id=partner, device_id_type=MESH)

    def out_local(h, k):
        src, dst = out_part(h, k)
        return pltpu.make_async_copy(src, dst, out_send.at[h, k])

    for h in range(halves):
        wait_halo(0, h)
    for k in range(local // 2):
        if k in (1, 2):
            pass_on(chunks - 3 + k, chunks - 2 + k)
        for other in (False, True):
            if other:
                @pl.when(away)
                def _():
                    for q in (2 * k, 2 * k + 1):
                        forward(q, mine=False).wait_recv()
            row = local - 1 - 2 * k - (1 - y % 2 if other else y % 2)
            first_row(row)
        if 2 * k + 2 == REACH_LO:
            for h in range(halves):
                start_up(1, h)
    for h in range(halves):
        start_down(1, h)

    for d in range(1, DEG):
        for h in range(halves):
            wait_halo(d, h)
            if d < DEG - 1:
                apply_rows(d, h, local - REACH_LO, local)
                start_up(d + 1, h)
                apply_rows(d, h, 0, local - REACH_LO)
                start_down(d + 1, h)
            else:
                for k in range(pieces):
                    apply_rows(d, h, k * (local // pieces), (k + 1) * (local // pieces))

                    @pl.when(away)
                    def _():
                        out_remote(h, k).start()

                    @pl.when(home)
                    def _():
                        out_local(h, k).start()

    for k in range(groups):
        grp = (g + 1 + k) % groups
        for h in range(halves):
            @pl.when(jnp.logical_not(jnp.logical_and(home, grp == g)))
            def _():
                a2a(grp, h).wait_send()
    for d in range(DEG):
        for h in range(halves):
            @pl.when(has_up)
            def _():
                up_copy(d, h).wait_send()

            @pl.when(has_low)
            def _():
                down_copy(d, h).wait_send()

    @pl.when(away)
    def _():
        for k in range(chunks):
            direct(k).wait_send()
            forward(k).wait_send()
        for h in range(halves):
            for k in range(pieces):
                out_remote(h, k).wait()

    @pl.when(home)
    def _():
        for h in range(halves):
            for k in range(pieces):
                out_local(h, k).wait()


def side_by_side(parts, whole):
    halves, rows, bs, width = parts.shape
    for h in range(halves):
        whole[:, h * width:(h + 1) * width] = parts[h].reshape(rows * bs, width)


def solution(mesh):
    rows, groups = mesh.shape["row"], mesh.shape["vec"]

    def per_device(vectors, rotation, blocks, columns):
        height, nv = vectors.shape
        local, nnz, bs, _ = blocks.shape
        group_width = nv // groups
        width = min(group_width, LANES)
        halves = group_width // width
        pieces = 2
        tiles = height // bs
        bf16, f32 = jnp.bfloat16, jnp.float32
        dma = pltpu.SemaphoreType.DMA
        span = REACH_LO + local + REACH_HI
        flops = 2 * height * nv * nv + 2 * DEG * local * nnz * bs * bs * group_width
        out = pl.pallas_call(
            functools.partial(filter_kernel, rows, groups, halves, pieces),
            out_shape=jax.ShapeDtypeStruct((halves, local, bs, width), bf16),
            in_specs=[
                pl.BlockSpec(memory_space=pl.ANY),
                pl.BlockSpec(memory_space=pl.ANY),
                pl.BlockSpec(memory_space=pl.ANY),
                pl.BlockSpec(memory_space=pl.ANY),
            ],
            out_specs=pl.BlockSpec(memory_space=pl.ANY),
            scratch_shapes=(
                [pltpu.VMEM((span, bs, width), bf16)] * (DEG * halves)
                + [pltpu.VMEM((local, bs, width), f32)] * (2 * halves)
                + [pltpu.VMEM((local, bs, width), bf16)] * halves
                + [
                    pltpu.VMEM((height, nv), bf16),
                    pltpu.VMEM((nv, nv), bf16),
                    pltpu.VMEM((groups, halves, tiles, bs, width), bf16),
                    pltpu.VMEM((local, nnz, bs, bs), bf16),
                    pltpu.VMEM(columns.shape, jnp.int32),
                    pltpu.SMEM(columns.shape, jnp.int32),
                    dma((3 + groups,)),
                    dma, dma,
                    dma((groups, halves)), dma((groups, halves)),
                    dma((local,)), dma((local,)),
                    dma((local,)), dma((local,)),
                    dma((DEG, halves, 2)), dma((DEG, halves, 2)),
                    dma((halves, pieces)), dma((halves, pieces)),
                ]
            ),
            compiler_params=pltpu.CompilerParams(
                collective_id=0, has_side_effects=True, vmem_limit_bytes=127 * 2**19),
            cost_estimate=pl.CostEstimate(
                flops=flops, bytes_accessed=8 * 2**20, transcendentals=0),
        )(vectors, rotation, blocks, columns)
        return pl.pallas_call(
            side_by_side,
            grid=(2,),
            out_shape=jax.ShapeDtypeStruct((local * bs, group_width), bf16),
            in_specs=[pl.BlockSpec((halves, local // 2, bs, width), lambda i: (0, i, 0, 0))],
            out_specs=pl.BlockSpec((local // 2 * bs, group_width), lambda i: (i, 0)),
            compiler_params=pltpu.CompilerParams(vmem_limit_bytes=8 * 2**20),
        )(out)

    return jax.shard_map(
        per_device,
        mesh=mesh,
        in_specs=(P(("row", "vec"), None), P(), P("row", None, None, None), P("row", None)),
        out_specs=P("row", "vec"),
        check_vma=False,
    )
```

```python
import functools

import jax
import jax.numpy as jnp
from jax import lax
from jax.experimental import pallas as pl
from jax.experimental.pallas import tpu as pltpu
from jax.sharding import PartitionSpec as P

DEG = 4
REACH_LO = 6
REACH_HI = 2
LANES = 128
MESH = pl.DeviceIdType.MESH


def filter_kernel(
    rows, groups, halves,
    vec_hbm, rot_hbm, blk_hbm, cols_in, out_hbm,
    *scratch,
):
    refs = list(scratch)
    take = lambda n: [refs.pop(0) for _ in range(n)]
    ext = [take(halves) for _ in range(DEG)]
    state = [take(halves) for _ in range(2)]
    res = take(halves)
    vec_v, rot_v, sendbuf, blk_v, cols_v, cols_s = take(6)
    (load_sem, cols_send, cols_recv, a2a_send, a2a_recv, blk_send, blk_recv,
     fwd_send, fwd_recv, halo_send, halo_recv, out_send, out_recv) = take(13)

    local, nnz, bs, _ = blk_v.shape
    span = ext[0][0].shape[0]
    tiles, width = sendbuf.shape[2], sendbuf.shape[4]
    chunks = local

    r, v = lax.axis_index("row"), lax.axis_index("vec")
    z, x = r // 2, r % 2
    y, c = v // 2, v % 2
    s, g = 2 * z + c, 2 * y + x
    home = x == c
    away = x != c
    first = s * local

    def device_of(sup, grp):
        return (2 * (sup // 2) + grp % 2, 2 * (grp // 2) + sup % 2)

    partner = (2 * z + 1 - x, 2 * y + 1 - c)
    across = (r, 2 * (y + 1 - 2 * (y % 2)) + c)
    has_low, has_up = s > 0, s < rows - 1
    low, up = device_of(s - 1, g), device_of(s + 1, g)
    far_low = jnp.logical_and(has_low, c == 0)
    far_up = jnp.logical_and(has_up, c == 1)

    barrier = pltpu.get_barrier_semaphore()
    for k in range(1, 2 * groups):
        q = (x * groups + v + k) % (2 * groups)
        pl.semaphore_signal(
            barrier, inc=1, device_id=(2 * z + q // groups, q % groups), device_id_type=MESH)

    @pl.when(far_low)
    def _():
        pl.semaphore_signal(barrier, inc=1, device_id=low, device_id_type=MESH)

    @pl.when(far_up)
    def _():
        pl.semaphore_signal(barrier, inc=1, device_id=up, device_id_type=MESH)

    vec_copy = pltpu.make_async_copy(vec_hbm, vec_v, load_sem.at[0])
    vec_copy.start()
    rot_copies = []
    for k in range(groups):
        cols = pl.ds(pl.multiple_of(((g + 1 + k) % groups) * (halves * width), LANES), halves * width)
        rot_copies.append(
            pltpu.make_async_copy(rot_hbm.at[:, cols], rot_v.at[:, cols], load_sem.at[3 + k]))
        rot_copies[-1].start()
    blk_copy = pltpu.make_async_copy(blk_hbm, blk_v, load_sem.at[1])

    @pl.when(home)
    def _():
        blk_copy.start()

    layers = jnp.where(jnp.logical_or(far_low, far_up), 1, 0)
    pl.semaphore_wait(barrier, 2 * groups - 1 + layers)

    cols_copy = pltpu.make_async_remote_copy(
        src_ref=cols_in, dst_ref=cols_v, send_sem=cols_send, recv_sem=cols_recv,
        device_id=partner, device_id_type=MESH)

    pairs = local // 2

    def pair_at(k, parity):
        return k + parity * (pairs - 1 - 2 * k)

    def chunk(q, side, parity):
        row = 2 * pair_at(q // 2, parity) + side
        return (pl.ds(row, 1), pl.ds((q % 2) * (nnz // 2), nnz // 2))

    def direct(q):
        part = chunk(q, y % 2, 1 - c)
        return pltpu.make_async_remote_copy(
            src_ref=blk_hbm.at[part], dst_ref=blk_v.at[part],
            send_sem=blk_send.at[q], recv_sem=blk_recv.at[q],
            device_id=partner, device_id_type=MESH)

    def forward(q, mine=True):
        part = chunk(q, y % 2 if mine else 1 - y % 2, c)
        return pltpu.make_async_remote_copy(
            src_ref=blk_v.at[part], dst_ref=blk_v.at[part],
            send_sem=fwd_send.at[q], recv_sem=fwd_recv.at[q],
            device_id=across, device_id_type=MESH)

    def start_direct(lo, hi):
        @pl.when(away)
        def _():
            for q in range(lo, hi):
                direct(q).start()

    def pass_on(lo, hi):
        @pl.when(away)
        def _():
            for q in range(lo, hi):
                direct(q).wait_recv()
                forward(q).start()

    @pl.when(away)
    def _():
        cols_copy.start()

    start_direct(0, 2)

    def a2a(grp, h):
        return pltpu.make_async_remote_copy(
            src_ref=sendbuf.at[grp, h],
            dst_ref=ext[0][h].at[pl.ds(REACH_LO + v * tiles, tiles)],
            send_sem=a2a_send.at[grp, h], recv_sem=a2a_recv.at[v, h],
            device_id=device_of(r, grp), device_id_type=MESH)

    vec_copy.wait()
    for k in range(groups):
        rot_copies[k].wait()
        grp = (g + 1 + k) % groups
        cols = pl.ds(pl.multiple_of(grp * (halves * width), LANES), halves * width)
        piece = jnp.dot(vec_v[...], rot_v[:, cols], preferred_element_type=jnp.float32)
        piece = piece.astype(jnp.bfloat16)
        own = jnp.logical_and(home, grp == g)
        for h in range(halves):
            part = piece[:, h * width:(h + 1) * width].reshape(tiles, bs, width)

            @pl.when(own)
            def _():
                ext[0][h][pl.ds(REACH_LO + v * tiles, tiles)] = part

            @pl.when(jnp.logical_not(own))
            def _():
                sendbuf[grp, h] = part
                a2a(grp, h).start()

    start_direct(2, 4)
    pass_on(0, 2)

    ups = REACH_LO // 2

    def up_copy(d, h, p):
        return pltpu.make_async_remote_copy(
            src_ref=ext[d][h].at[pl.ds(local + 2 * p, 2)],
            dst_ref=ext[d][h].at[pl.ds(2 * p, 2)],
            send_sem=halo_send.at[d, h, p], recv_sem=halo_recv.at[d, h, p],
            device_id=up, device_id_type=MESH)

    def down_copy(d, h):
        return pltpu.make_async_remote_copy(
            src_ref=ext[d][h].at[pl.ds(REACH_LO, REACH_HI)],
            dst_ref=ext[d][h].at[pl.ds(REACH_LO + local, REACH_HI)],
            send_sem=halo_send.at[d, h, ups], recv_sem=halo_recv.at[d, h, ups],
            device_id=low, device_id_type=MESH)

    def send_pair(d, h, pair):
        if pair * 2 < REACH_HI:
            @pl.when(has_low)
            def _():
                down_copy(d, h).start()
        if pair >= pairs - ups:
            @pl.when(has_up)
            def _():
                up_copy(d, h, pair - (pairs - ups)).start()

    def send_after(d, h, k):
        @pl.when(c == 0)
        def _():
            send_pair(d, h, k)

        @pl.when(c == 1)
        def _():
            send_pair(d, h, pairs - 1 - k)

    def wait_halo(d, h):
        @pl.when(has_low)
        def _():
            for p in range(ups):
                up_copy(d, h, p).wait_recv()

        @pl.when(has_up)
        def _():
            down_copy(d, h).wait_recv()

    for h in range(halves):
        for src in range(groups):
            @pl.when(jnp.logical_not(jnp.logical_and(home, v == src)))
            def _():
                pltpu.make_async_remote_copy(
                    src_ref=sendbuf.at[0, h],
                    dst_ref=ext[0][h].at[pl.ds(REACH_LO + src * tiles, tiles)],
                    send_sem=a2a_send.at[0, h], recv_sem=a2a_recv.at[src, h],
                    device_id=partner, device_id_type=MESH).wait_recv()
        for k in range(pairs):
            send_after(0, h, k)
        if h == 0:
            start_direct(4, 6)
    start_direct(6, chunks)
    pass_on(2, 6)

    @pl.when(away)
    def _():
        cols_copy.wait()
        to_smem = pltpu.make_async_copy(cols_v, cols_s, load_sem.at[2])
        to_smem.start()
        to_smem.wait()

    @pl.when(home)
    def _():
        to_smem = pltpu.make_async_copy(cols_in, cols_s, load_sem.at[2])
        to_smem.start()
        to_smem.wait()
        blk_copy.wait()

    def product(d, parts, i):
        lhs = jnp.concatenate([blk_v[i, j] for j in range(nnz)], axis=1)
        tile = [jnp.clip(cols_s[i, j] - first + REACH_LO, 0, span - 1) for j in range(nnz)]
        rhs = [jnp.concatenate([ext[d][h][t] for t in tile], axis=0) for h in parts]
        rhs = rhs[0] if len(parts) == 1 else jnp.concatenate(rhs, axis=1)
        return jnp.dot(lhs, rhs, preferred_element_type=jnp.float32)

    def first_row(i):
        acc = product(0, range(halves), i)
        for h in range(halves):
            old = ext[0][h][REACH_LO + i].astype(jnp.float32)
            new = (acc[:, h * width:(h + 1) * width] - 0.25 * old) / 2.0
            state[0][h][i] = new
            ext[1][h][REACH_LO + i] = new.astype(jnp.bfloat16)

    def one_row(d, h, i):
        acc = product(d, (h,), i)
        cur = state[(d - 1) % 2][h][i]
        if d == 1:
            prev = ext[0][h][REACH_LO + i].astype(jnp.float32)
        else:
            prev = state[d % 2][h][i]
        new = (acc - 0.25 * cur) - prev
        if d < DEG - 1:
            state[d % 2][h][i] = new
            ext[d + 1][h][REACH_LO + i] = new.astype(jnp.bfloat16)
        else:
            res[h][i] = new.astype(jnp.bfloat16)

    def out_part(h, k, parity=c):
        part = pl.ds(2 * pair_at(k, parity), 2)
        return res[h].at[part], out_hbm.at[part, :, pl.ds(h * width, width)]

    def out_remote(h, k):
        src, dst = out_part(h, k)
        return pltpu.make_async_remote_copy(
            src_ref=src, dst_ref=dst, send_sem=out_send.at[h, k], recv_sem=out_recv.at[h, k],
            device_id=partner, device_id_type=MESH)

    def out_local(h, k):
        src, dst = out_part(h, k)
        return pltpu.make_async_copy(src, dst, out_send.at[h, k])

    for h in range(halves):
        wait_halo(0, h)
    for k in range(pairs):
        if k == pairs - 2:
            pass_on(chunks - 2, chunks)
        for side in range(2):
            if side == 1:
                @pl.when(away)
                def _():
                    for q in (2 * k, 2 * k + 1):
                        forward(q, mine=False).wait_recv()
            first_row(2 * pair_at(k, c) + (1 - y % 2 if side else y % 2))
        for h in range(halves):
            send_after(1, h, k)

    for d in range(1, DEG):
        for h in range(halves):
            wait_halo(d, h)
            for k in range(pairs):
                for side in range(2):
                    one_row(d, h, 2 * pair_at(k, c) + side)
                if d < DEG - 1:
                    send_after(d + 1, h, k)
                else:
                    @pl.when(away)
                    def _():
                        out_remote(h, k).start()

                    @pl.when(home)
                    def _():
                        out_local(h, k).start()

    for k in range(groups):
        grp = (g + 1 + k) % groups
        for h in range(halves):
            @pl.when(jnp.logical_not(jnp.logical_and(home, grp == g)))
            def _():
                a2a(grp, h).wait_send()
    for d in range(DEG):
        for h in range(halves):
            @pl.when(has_up)
            def _():
                for p in range(ups):
                    up_copy(d, h, p).wait_send()

            @pl.when(has_low)
            def _():
                down_copy(d, h).wait_send()

    @pl.when(away)
    def _():
        for k in range(chunks):
            direct(k).wait_send()
            forward(k).wait_send()
        for h in range(halves):
            for k in range(pairs):
                out_remote(h, k).wait()

    @pl.when(home)
    def _():
        for h in range(halves):
            for k in range(pairs):
                out_local(h, k).wait()


def solution(mesh):
    rows, groups = mesh.shape["row"], mesh.shape["vec"]

    def per_device(vectors, rotation, blocks, columns):
        height, nv = vectors.shape
        local, nnz, bs, _ = blocks.shape
        group_width = nv // groups
        width = min(group_width, LANES)
        halves = group_width // width
        tiles = height // bs
        bf16, f32 = jnp.bfloat16, jnp.float32
        dma = pltpu.SemaphoreType.DMA
        span = REACH_LO + local + REACH_HI
        flops = 2 * height * nv * nv + 2 * DEG * local * nnz * bs * bs * group_width
        out = pl.pallas_call(
            functools.partial(filter_kernel, rows, groups, halves),
            out_shape=jax.ShapeDtypeStruct((local, bs, group_width), bf16),
            in_specs=[
                pl.BlockSpec(memory_space=pl.ANY),
                pl.BlockSpec(memory_space=pl.ANY),
                pl.BlockSpec(memory_space=pl.ANY),
                pl.BlockSpec(memory_space=pl.ANY),
            ],
            out_specs=pl.BlockSpec(memory_space=pl.ANY),
            scratch_shapes=(
                [pltpu.VMEM((span, bs, width), bf16)] * (DEG * halves)
                + [pltpu.VMEM((local, bs, width), f32)] * (2 * halves)
                + [pltpu.VMEM((local, bs, width), bf16)] * halves
                + [
                    pltpu.VMEM((height, nv), bf16),
                    pltpu.VMEM((nv, nv), bf16),
                    pltpu.VMEM((groups, halves, tiles, bs, width), bf16),
                    pltpu.VMEM((local, nnz, bs, bs), bf16),
                    pltpu.VMEM(columns.shape, jnp.int32),
                    pltpu.SMEM(columns.shape, jnp.int32),
                    dma((3 + groups,)),
                    dma, dma,
                    dma((groups, halves)), dma((groups, halves)),
                    dma((local,)), dma((local,)),
                    dma((local,)), dma((local,)),
                    dma((DEG, halves, REACH_LO // 2 + 1)), dma((DEG, halves, REACH_LO // 2 + 1)),
                    dma((halves, local // 2)), dma((halves, local // 2)),
                ]
            ),
            compiler_params=pltpu.CompilerParams(
                collective_id=0, has_side_effects=True, vmem_limit_bytes=253 * 2**18),
            cost_estimate=pl.CostEstimate(
                flops=flops, bytes_accessed=8 * 2**20, transcendentals=0),
        )(vectors, rotation, blocks, columns)
        return out.reshape(local * bs, group_width)

    return jax.shard_map(
        per_device,
        mesh=mesh,
        in_specs=(P(("row", "vec"), None), P(), P("row", None, None, None), P("row", None)),
        out_specs=P("row", "vec"),
        check_vma=False,
    )
```

```python
import functools

import jax
import jax.numpy as jnp
from jax import lax
from jax.experimental import pallas as pl
from jax.experimental.pallas import tpu as pltpu
from jax.sharding import PartitionSpec as P

DEG = 4
REACH_LO = 6
REACH_HI = 2
LANES = 128
MESH = pl.DeviceIdType.MESH


def filter_kernel(
    rows, groups, halves,
    vec_hbm, rot_hbm, blk_hbm, cols_in, out_hbm,
    *scratch,
):
    refs = list(scratch)
    take = lambda n: [refs.pop(0) for _ in range(n)]
    ext = [take(halves) for _ in range(DEG)]
    state = [take(halves) for _ in range(2)]
    res = take(halves)
    vec_v, rot_v, sendbuf, blk_v, cols_v, cols_s = take(6)
    (load_sem, cols_send, cols_recv, a2a_send, a2a_recv, blk_send, blk_recv,
     fwd_send, fwd_recv, halo_send, halo_recv, out_send, out_recv) = take(13)

    local, nnz, bs, _ = blk_v.shape
    span = ext[0][0].shape[0]
    tiles, width = sendbuf.shape[2], sendbuf.shape[4]
    chunks = local

    r, v = lax.axis_index("row"), lax.axis_index("vec")
    z, x = r // 2, r % 2
    y, c = v // 2, v % 2
    s, g = 2 * z + c, 2 * y + x
    home = x == c
    away = x != c
    first = s * local

    def device_of(sup, grp):
        return (2 * (sup // 2) + grp % 2, 2 * (grp // 2) + sup % 2)

    partner = (2 * z + 1 - x, 2 * y + 1 - c)
    across = (r, 2 * (y + 1 - 2 * (y % 2)) + c)
    has_low, has_up = s > 0, s < rows - 1
    low, up = device_of(s - 1, g), device_of(s + 1, g)
    far_low = jnp.logical_and(has_low, c == 0)
    far_up = jnp.logical_and(has_up, c == 1)

    barrier = pltpu.get_barrier_semaphore()
    for k in range(1, 2 * groups):
        q = (x * groups + v + k) % (2 * groups)
        pl.semaphore_signal(
            barrier, inc=1, device_id=(2 * z + q // groups, q % groups), device_id_type=MESH)

    @pl.when(far_low)
    def _():
        pl.semaphore_signal(barrier, inc=1, device_id=low, device_id_type=MESH)

    @pl.when(far_up)
    def _():
        pl.semaphore_signal(barrier, inc=1, device_id=up, device_id_type=MESH)

    vec_copy = pltpu.make_async_copy(vec_hbm, vec_v, load_sem.at[0])
    vec_copy.start()
    rot_copies = []
    for k in range(groups):
        cols = pl.ds(pl.multiple_of(((g + 1 + k) % groups) * (halves * width), LANES), halves * width)
        rot_copies.append(
            pltpu.make_async_copy(rot_hbm.at[:, cols], rot_v.at[:, cols], load_sem.at[3 + k]))
        rot_copies[-1].start()
    blk_copy = pltpu.make_async_copy(blk_hbm, blk_v, load_sem.at[1])

    @pl.when(home)
    def _():
        blk_copy.start()

    layers = jnp.where(jnp.logical_or(far_low, far_up), 1, 0)
    pl.semaphore_wait(barrier, 2 * groups - 1 + layers)

    cols_copy = pltpu.make_async_remote_copy(
        src_ref=cols_in, dst_ref=cols_v, send_sem=cols_send, recv_sem=cols_recv,
        device_id=partner, device_id_type=MESH)

    pairs = local // 2

    def pair_at(k, parity):
        return k + parity * (pairs - 1 - 2 * k)

    def chunk(q, side, parity):
        row = 2 * pair_at(q // 2, parity) + side
        return (pl.ds(row, 1), pl.ds((q % 2) * (nnz // 2), nnz // 2))

    def direct(q):
        part = chunk(q, y % 2, 1 - c)
        return pltpu.make_async_remote_copy(
            src_ref=blk_hbm.at[part], dst_ref=blk_v.at[part],
            send_sem=blk_send.at[q], recv_sem=blk_recv.at[q],
            device_id=partner, device_id_type=MESH)

    def forward(q, mine=True):
        part = chunk(q, y % 2 if mine else 1 - y % 2, c)
        return pltpu.make_async_remote_copy(
            src_ref=blk_v.at[part], dst_ref=blk_v.at[part],
            send_sem=fwd_send.at[q], recv_sem=fwd_recv.at[q],
            device_id=across, device_id_type=MESH)

    def start_direct(lo, hi):
        @pl.when(away)
        def _():
            for q in range(lo, hi):
                direct(q).start()

    def pass_on(lo, hi):
        @pl.when(away)
        def _():
            for q in range(lo, hi):
                direct(q).wait_recv()
                forward(q).start()

    @pl.when(away)
    def _():
        cols_copy.start()

    start_direct(0, 2)

    def a2a(grp, h):
        return pltpu.make_async_remote_copy(
            src_ref=sendbuf.at[grp, h],
            dst_ref=ext[0][h].at[pl.ds(REACH_LO + v * tiles, tiles)],
            send_sem=a2a_send.at[grp, h], recv_sem=a2a_recv.at[v, h],
            device_id=device_of(r, grp), device_id_type=MESH)

    vec_copy.wait()
    for k in range(groups):
        rot_copies[k].wait()
        grp = (g + 1 + k) % groups
        cols = pl.ds(pl.multiple_of(grp * (halves * width), LANES), halves * width)
        piece = jnp.dot(vec_v[...], rot_v[:, cols], preferred_element_type=jnp.float32)
        piece = piece.astype(jnp.bfloat16)
        own = jnp.logical_and(home, grp == g)
        for h in range(halves):
            part = piece[:, h * width:(h + 1) * width].reshape(tiles, bs, width)

            @pl.when(own)
            def _():
                ext[0][h][pl.ds(REACH_LO + v * tiles, tiles)] = part

            @pl.when(jnp.logical_not(own))
            def _():
                sendbuf[grp, h] = part
                a2a(grp, h).start()

    start_direct(2, 4)
    pass_on(0, 2)

    ups = REACH_LO // 2

    def up_copy(d, h, p):
        return pltpu.make_async_remote_copy(
            src_ref=ext[d][h].at[pl.ds(local + 2 * p, 2)],
            dst_ref=ext[d][h].at[pl.ds(2 * p, 2)],
            send_sem=halo_send.at[d, h, p], recv_sem=halo_recv.at[d, h, p],
            device_id=up, device_id_type=MESH)

    def down_copy(d, h):
        return pltpu.make_async_remote_copy(
            src_ref=ext[d][h].at[pl.ds(REACH_LO, REACH_HI)],
            dst_ref=ext[d][h].at[pl.ds(REACH_LO + local, REACH_HI)],
            send_sem=halo_send.at[d, h, ups], recv_sem=halo_recv.at[d, h, ups],
            device_id=low, device_id_type=MESH)

    def send_pair(d, h, pair):
        if pair * 2 < REACH_HI:
            @pl.when(has_low)
            def _():
                down_copy(d, h).start()
        if pair >= pairs - ups:
            @pl.when(has_up)
            def _():
                up_copy(d, h, pair - (pairs - ups)).start()

    def send_after(d, h, k):
        @pl.when(c == 0)
        def _():
            send_pair(d, h, k)

        @pl.when(c == 1)
        def _():
            send_pair(d, h, pairs - 1 - k)

    def wait_halo(d, h):
        @pl.when(has_low)
        def _():
            for p in range(ups):
                up_copy(d, h, p).wait_recv()

        @pl.when(has_up)
        def _():
            down_copy(d, h).wait_recv()

    for h in range(halves):
        for src in range(groups):
            @pl.when(jnp.logical_not(jnp.logical_and(home, v == src)))
            def _():
                pltpu.make_async_remote_copy(
                    src_ref=sendbuf.at[0, h],
                    dst_ref=ext[0][h].at[pl.ds(REACH_LO + src * tiles, tiles)],
                    send_sem=a2a_send.at[0, h], recv_sem=a2a_recv.at[src, h],
                    device_id=partner, device_id_type=MESH).wait_recv()
        for k in range(pairs):
            send_after(0, h, k)
        if h == 0:
            start_direct(4, 6)
    start_direct(6, chunks)
    pass_on(2, 6)

    @pl.when(away)
    def _():
        cols_copy.wait()
        to_smem = pltpu.make_async_copy(cols_v, cols_s, load_sem.at[2])
        to_smem.start()
        to_smem.wait()

    @pl.when(home)
    def _():
        to_smem = pltpu.make_async_copy(cols_in, cols_s, load_sem.at[2])
        to_smem.start()
        to_smem.wait()
        blk_copy.wait()

    def product(d, parts, i):
        lhs = jnp.concatenate([blk_v[i, j] for j in range(nnz)], axis=1)
        tile = [jnp.clip(cols_s[i, j] - first + REACH_LO, 0, span - 1) for j in range(nnz)]
        rhs = [jnp.concatenate([ext[d][h][t] for t in tile], axis=0) for h in parts]
        rhs = rhs[0] if len(parts) == 1 else jnp.concatenate(rhs, axis=1)
        return jnp.dot(lhs, rhs, preferred_element_type=jnp.float32)

    def first_row(i):
        acc = product(0, range(halves), i)
        for h in range(halves):
            old = ext[0][h][REACH_LO + i].astype(jnp.float32)
            new = (acc[:, h * width:(h + 1) * width] - 0.25 * old) / 2.0
            state[0][h][i] = new
            ext[1][h][REACH_LO + i] = new.astype(jnp.bfloat16)

    def one_row(d, h, i):
        acc = product(d, (h,), i)
        cur = state[(d - 1) % 2][h][i]
        if d == 1:
            prev = ext[0][h][REACH_LO + i].astype(jnp.float32)
        else:
            prev = state[d % 2][h][i]
        new = (acc - 0.25 * cur) - prev
        if d < DEG - 1:
            state[d % 2][h][i] = new
            ext[d + 1][h][REACH_LO + i] = new.astype(jnp.bfloat16)
        else:
            res[h][i] = new.astype(jnp.bfloat16)

    def out_part(h, k, parity=c):
        part = pl.ds(2 * pair_at(k, parity), 2)
        return res[h].at[part], out_hbm.at[part, :, pl.ds(h * width, width)]

    def out_remote(h, k):
        src, dst = out_part(h, k)
        return pltpu.make_async_remote_copy(
            src_ref=src, dst_ref=dst, send_sem=out_send.at[h, k], recv_sem=out_recv.at[h, k],
            device_id=partner, device_id_type=MESH)

    def out_local(h, k):
        src, dst = out_part(h, k)
        return pltpu.make_async_copy(src, dst, out_send.at[h, k])

    for h in range(halves):
        wait_halo(0, h)
    for k in range(pairs):
        if k == pairs - 2:
            pass_on(chunks - 2, chunks)
        for side in range(2):
            if side == 1:
                @pl.when(away)
                def _():
                    for q in (2 * k, 2 * k + 1):
                        forward(q, mine=False).wait_recv()
            first_row(2 * pair_at(k, c) + (1 - y % 2 if side else y % 2))
        for h in range(halves):
            send_after(1, h, k)

    for d in range(1, DEG):
        for h in range(halves):
            wait_halo(d, h)
            for k in range(pairs):
                for side in range(2):
                    one_row(d, h, 2 * pair_at(k, c) + side)
                if d < DEG - 1:
                    send_after(d + 1, h, k)
                else:
                    @pl.when(away)
                    def _():
                        out_remote(h, k).start()

                    @pl.when(home)
                    def _():
                        out_local(h, k).start()

    for k in range(groups):
        grp = (g + 1 + k) % groups
        for h in range(halves):
            @pl.when(jnp.logical_not(jnp.logical_and(home, grp == g)))
            def _():
                a2a(grp, h).wait_send()
    for d in range(DEG):
        for h in range(halves):
            @pl.when(has_up)
            def _():
                for p in range(ups):
                    up_copy(d, h, p).wait_send()

            @pl.when(has_low)
            def _():
                down_copy(d, h).wait_send()

    @pl.when(away)
    def _():
        for k in range(chunks):
            direct(k).wait_send()
            forward(k).wait_send()
        for h in range(halves):
            for k in range(pairs):
                out_remote(h, k).wait()

    @pl.when(home)
    def _():
        for h in range(halves):
            for k in range(pairs):
                out_local(h, k).wait()


def hand_over(src, dst, sems):
    copies = [pltpu.make_async_copy(src.at[i], dst.at[i], sems.at[i]) for i in range(src.shape[0])]
    for copy in copies:
        copy.start()
    for copy in copies:
        copy.wait()


def solution(mesh):
    rows, groups = mesh.shape["row"], mesh.shape["vec"]

    def per_device(vectors, rotation, blocks, columns):
        height, nv = vectors.shape
        local, nnz, bs, _ = blocks.shape
        group_width = nv // groups
        width = min(group_width, LANES)
        halves = group_width // width
        tiles = height // bs
        bf16, f32 = jnp.bfloat16, jnp.float32
        dma = pltpu.SemaphoreType.DMA
        span = REACH_LO + local + REACH_HI
        flops = 2 * height * nv * nv + 2 * DEG * local * nnz * bs * bs * group_width
        out = pl.pallas_call(
            functools.partial(filter_kernel, rows, groups, halves),
            out_shape=jax.ShapeDtypeStruct((local, bs, group_width), bf16),
            in_specs=[
                pl.BlockSpec(memory_space=pl.ANY),
                pl.BlockSpec(memory_space=pl.ANY),
                pl.BlockSpec(memory_space=pl.ANY),
                pl.BlockSpec(memory_space=pl.ANY),
            ],
            out_specs=pl.BlockSpec(memory_space=pl.ANY),
            scratch_shapes=(
                [pltpu.VMEM((span, bs, width), bf16)] * (DEG * halves)
                + [pltpu.VMEM((local, bs, width), f32)] * (2 * halves)
                + [pltpu.VMEM((local, bs, width), bf16)] * halves
                + [
                    pltpu.VMEM((height, nv), bf16),
                    pltpu.VMEM((nv, nv), bf16),
                    pltpu.VMEM((groups, halves, tiles, bs, width), bf16),
                    pltpu.VMEM((local, nnz, bs, bs), bf16),
                    pltpu.VMEM(columns.shape, jnp.int32),
                    pltpu.SMEM(columns.shape, jnp.int32),
                    dma((3 + groups,)),
                    dma, dma,
                    dma((groups, halves)), dma((groups, halves)),
                    dma((local,)), dma((local,)),
                    dma((local,)), dma((local,)),
                    dma((DEG, halves, REACH_LO // 2 + 1)), dma((DEG, halves, REACH_LO // 2 + 1)),
                    dma((halves, local // 2)), dma((halves, local // 2)),
                ]
            ),
            compiler_params=pltpu.CompilerParams(
                collective_id=0, has_side_effects=True, vmem_limit_bytes=253 * 2**18),
            cost_estimate=pl.CostEstimate(
                flops=flops, bytes_accessed=8 * 2**20, transcendentals=0),
        )(vectors, rotation, blocks, columns)
        out = pl.pallas_call(
            hand_over,
            out_shape=jax.ShapeDtypeStruct(out.shape, bf16),
            in_specs=[pl.BlockSpec(memory_space=pl.ANY)],
            out_specs=pl.BlockSpec(memory_space=pl.ANY),
            scratch_shapes=[dma((local,))],
            compiler_params=pltpu.CompilerParams(vmem_limit_bytes=127 * 2**19),
        )(out)
        return out.reshape(local * bs, group_width)

    return jax.shard_map(
        per_device,
        mesh=mesh,
        in_specs=(P(("row", "vec"), None), P(), P("row", None, None, None), P("row", None)),
        out_specs=P("row", "vec"),
        check_vma=False,
    )
```
